32 devices in a mesh: exp: 8 (over z, x), rep: 4 (over y, core).
Axes of the slice: x: 2, y: 2, z: 4, core: 2. Of those that a mesh axis runs over, the one named last changes fastest.
Arguments:
- images: bfloat16 [64, 256, 1024], P(('exp', 'rep')), may hold values from -12 to 12
- router: float32 [1024, 32], P(('exp', 'rep')), may hold values from -4 to 4
- w_in: bfloat16 [32, 1024, 2560], P(('exp', 'rep')), may hold values from -0.1875 to 0.1875
- w_out: bfloat16 [32, 2560, 1024], P(('exp', 'rep')), may hold values from -0.125 to 0.125
- out_grad: bfloat16 [64, 256, 1024], P(('exp', 'rep')), may hold values from -6 to 6
Outputs:
- images_grad: bfloat16 [64, 256, 1024], P(('exp', 'rep'))
- w_in_grad: bfloat16 [32, 1024, 2560], P(('exp', 'rep'))
- w_out_grad: bfloat16 [32, 2560, 1024], P(('exp', 'rep'))
- router_grad: float32 [1024, 32], P(('exp', 'rep'))
The draws below stay inside these ranges and needn't reach their ends.
All inputs are finite; a program needn't handle non-finite values.
Results may differ from the reference program's by a relative error of at most 0.012.
The reference program's roundings to bfloat16 on the way (of `router_low`, `slot_in`, `slot_grad`, `hidden`, `slot_out`, `pre_grad`, `slot_dx` and `logit_grad`) count: a program that leaves them out, or rounds other values in their place, can miss the bound.
Values may be sent and summed in bfloat16 or wider, within the bound.
A program may use at most 128 MiB of HBM per device.

```python
import jax
import jax.numpy as jnp
from jax import lax

D = 1024
FF = 2560
TOK = 256
EXPERTS = 32
IMAGES = 64


def draw_router(key, part):
    key = jax.random.fold_in(key, 11)
    return jnp.clip(jax.random.normal(key, (D, EXPERTS), jnp.float32), -4.0, 4.0)


def draw_images(key, part):
    key = jax.random.fold_in(key, 23)
    sub_keys = jax.random.split(key, 2)
    scales = 0.5 * 6.0 ** jax.random.uniform(sub_keys[0], (IMAGES, TOK, 1), jnp.float32)
    return jnp.clip(scales * jax.random.normal(sub_keys[1], (IMAGES, TOK, D), jnp.float32), -12.0, 12.0).astype(jnp.bfloat16)


def levels(rng, dims, cuts, smallest, top_value):
    def one(position, shards_of):
        steps = jax.random.uniform(jax.random.fold_in(jax.random.fold_in(rng, 6), position), (shards_of,), jnp.float32, smallest / len(cuts), top_value / len(cuts))
        return jnp.repeat(jnp.exp(steps), dims[position] // shards_of).reshape((-1,) + (1,) * (len(dims) - position - 1))

    level = one(*cuts[0])
    for cut in cuts[1:]:
        level = level * one(*cut)
    return level


def noise(rng, dims, deviation, most, cuts=(), held_as=jnp.bfloat16):
    values = deviation * jax.random.normal(rng, dims, jnp.float32)
    if cuts:
        values = values * levels(rng, dims, cuts, -0.22, 0.18)
    return jnp.clip(values, -most, most).astype(held_as)


def setup_inputs(seed: int = 0) -> dict:
    arg_keys = jax.random.split(jax.random.key(seed), 6)
    return {
        "images": draw_images(jax.random.fold_in(arg_keys[5], 71), 0),
        "router": draw_router(jax.random.fold_in(arg_keys[5], 71), 0),
        "w_in": noise(arg_keys[2], (EXPERTS, D, FF), D ** -0.5, 0.1875, ((0, 32),)),
        "w_out": noise(arg_keys[3], (EXPERTS, FF, D), FF ** -0.5, 0.125, ((0, 32),)),
        "out_grad": noise(arg_keys[4], (IMAGES, TOK, D), 1.0, 6.0, ((0, 32),)),
    }


LOGIT_SCALE = 2.0
EPS = 1e-06
SQRT_HALF = 0.7071067811865476
INV_ROOT = 0.3989422804014327

def gelu_parts(pre_value):
    cumulative = 0.5 * (1.0 + lax.erf(pre_value * SQRT_HALF))
    gelu_slope = cumulative + pre_value * jnp.exp(-0.5 * pre_value * pre_value) * INV_ROOT
    return (pre_value * cumulative, gelu_slope)

def expert_pass(operands):
    slot_rows, slot_grads, weight_in, weight_out = operands
    pre_act = jnp.dot(slot_rows, weight_in, preferred_element_type=jnp.float32)
    activated, gelu_slope = gelu_parts(pre_act)
    hidden = activated.astype(jnp.bfloat16)
    slot_out = jnp.dot(hidden, weight_out, preferred_element_type=jnp.float32).astype(jnp.bfloat16)
    hidden_grad = jnp.dot(slot_grads, weight_out.T, preferred_element_type=jnp.float32)
    pre_grad = (hidden_grad * gelu_slope).astype(jnp.bfloat16)
    grad_out = jnp.dot(hidden.T, slot_grads, preferred_element_type=jnp.float32).astype(jnp.bfloat16)
    grad_in = jnp.dot(slot_rows.T, pre_grad, preferred_element_type=jnp.float32).astype(jnp.bfloat16)
    slot_dx = jnp.dot(pre_grad, weight_in.T, preferred_element_type=jnp.float32).astype(jnp.bfloat16)
    return (slot_out, slot_dx, grad_in, grad_out)

def reference(images, router, w_in, w_out, out_grad):
    inv_norm = lax.rsqrt(lax.optimization_barrier(jnp.sum(router * router, axis=0)) + EPS)
    router_hat = router * inv_norm
    router_low = router_hat.astype(jnp.bfloat16)
    low_wide = lax.optimization_barrier(router_low).astype(jnp.float32)
    images_wide = images.astype(jnp.float32)
    grad_wide = out_grad.astype(jnp.float32)
    logits = LOGIT_SCALE * jnp.einsum('btd,de->bte', images_wide, low_wide)
    dispatch = jax.nn.softmax(logits, axis=1)
    combine = jax.nn.softmax(logits, axis=2)
    dispatch_low = dispatch.astype(jnp.bfloat16)
    combine_low = combine.astype(jnp.bfloat16)
    slot_in = jnp.einsum('bte,btd->bed', dispatch_low.astype(jnp.float32), images_wide).astype(jnp.bfloat16)
    slot_grad = jnp.einsum('bte,btd->bed', combine_low.astype(jnp.float32), grad_wide).astype(jnp.bfloat16)
    results = lax.map(expert_pass, (jnp.transpose(slot_in, (1, 0, 2)), jnp.transpose(slot_grad, (1, 0, 2)), w_in, w_out))
    slot_out = jnp.transpose(results[0], (1, 0, 2)).astype(jnp.float32)
    slot_dx = jnp.transpose(results[1], (1, 0, 2)).astype(jnp.float32)
    combine_grad = jnp.einsum('btd,bed->bte', grad_wide, slot_out)
    grad_combine = combine * (combine_grad - lax.optimization_barrier(jnp.sum(combine * combine_grad, axis=2, keepdims=True)))
    dispatch_grad = jnp.einsum('btd,bed->bte', images_wide, slot_dx)
    grad_dispatch = dispatch * (dispatch_grad - lax.optimization_barrier(jnp.sum(dispatch * dispatch_grad, axis=1, keepdims=True)))
    logit_grad = (LOGIT_SCALE * (grad_combine + grad_dispatch)).astype(jnp.bfloat16)
    logit_wide = logit_grad.astype(jnp.float32)
    images_grad = (jnp.einsum('bte,bed->btd', dispatch_low.astype(jnp.float32), slot_dx) + jnp.einsum('bte,de->btd', logit_wide, low_wide)).astype(jnp.bfloat16)
    hat_grad = jnp.einsum('btd,bte->de', images_wide, logit_wide)
    moment = lax.optimization_barrier(jnp.sum(low_wide * hat_grad, axis=0))
    router_grad = (hat_grad - router_hat * moment) * inv_norm
    return (images_grad, results[2], results[3], router_grad)
```

```python
import jax
import jax.numpy as jnp
from jax import lax
from jax.sharding import PartitionSpec as P

LOGIT_SCALE = 2.0
EPS = 1e-06
SQRT_HALF = 0.7071067811865476
INV_ROOT = 0.3989422804014327


def gelu_parts(pre_value):
    cumulative = 0.5 * (1.0 + lax.erf(pre_value * SQRT_HALF))
    gelu_slope = cumulative + pre_value * jnp.exp(-0.5 * pre_value * pre_value) * INV_ROOT
    return (pre_value * cumulative, gelu_slope)


def contract_last(left_side, right_side):
    return lax.dot_general(
        left_side, right_side, (((1,), (1,)), ((), ())), preferred_element_type=jnp.float32
    )


def contract_first(left_side, right_side):
    return lax.dot_general(
        left_side, right_side, (((0,), (0,)), ((), ())), preferred_element_type=jnp.float32
    )


def expert_pass(slot_rows, slot_grads, weight_in, weight_out):
    pre_act = jnp.dot(slot_rows, weight_in, preferred_element_type=jnp.float32)
    activated, gelu_slope = gelu_parts(pre_act)
    hidden = activated.astype(jnp.bfloat16)
    slot_out = jnp.dot(hidden, weight_out, preferred_element_type=jnp.float32).astype(jnp.bfloat16)
    hidden_grad = contract_last(slot_grads, weight_out)
    pre_grad = (hidden_grad * gelu_slope).astype(jnp.bfloat16)
    grad_out = contract_first(hidden, slot_grads).astype(jnp.bfloat16)
    grad_in = contract_first(slot_rows, pre_grad).astype(jnp.bfloat16)
    slot_dx = contract_last(pre_grad, weight_in).astype(jnp.bfloat16)
    return (slot_out, slot_dx, grad_in, grad_out)


def per_device(images, router, w_in, w_out, out_grad):
    model_width = images.shape[2]
    devices = lax.axis_size(("exp", "rep"))
    router_whole = lax.all_to_all(
        jnp.broadcast_to(router[None], (devices,) + router.shape),
        ("exp", "rep"),
        split_axis=0,
        concat_axis=0,
        tiled=True,
    ).reshape(model_width, -1)
    inv_norm = lax.rsqrt(jnp.sum(router_whole * router_whole, axis=0) + EPS)
    router_low = (router_whole * inv_norm).astype(jnp.bfloat16)
    logits = LOGIT_SCALE * jnp.einsum(
        "btd,de->bte", images, router_low, preferred_element_type=jnp.float32
    )
    dispatch = jax.nn.softmax(logits, axis=1)
    combine = jax.nn.softmax(logits, axis=2)
    dispatch_low = dispatch.astype(jnp.bfloat16)
    combine_low = combine.astype(jnp.bfloat16)
    slot_in = jnp.einsum(
        "bte,btd->bed", dispatch_low, images, preferred_element_type=jnp.float32
    ).astype(jnp.bfloat16)
    slot_grad = jnp.einsum(
        "bte,btd->bed", combine_low, out_grad, preferred_element_type=jnp.float32
    ).astype(jnp.bfloat16)
    paired = jnp.stack((slot_in, slot_grad), axis=0)
    arrived = lax.all_to_all(paired, ("exp", "rep"), split_axis=2, concat_axis=1, tiled=True)
    arrived = arrived.reshape(2, -1, model_width)
    slot_out, slot_dx, grad_in, grad_out = expert_pass(arrived[0], arrived[1], w_in[0], w_out[0])
    results = jnp.stack((slot_out, slot_dx), axis=0)
    returned = lax.all_to_all(
        results[:, :, None, :], ("exp", "rep"), split_axis=1, concat_axis=2, tiled=True
    )
    combine_grad = jnp.einsum(
        "btd,bed->bte", out_grad, returned[0], preferred_element_type=jnp.float32
    )
    grad_combine = combine * (combine_grad - jnp.sum(combine * combine_grad, axis=2, keepdims=True))
    dispatch_grad = jnp.einsum(
        "btd,bed->bte", images, returned[1], preferred_element_type=jnp.float32
    )
    grad_dispatch = dispatch * (
        dispatch_grad - jnp.sum(dispatch * dispatch_grad, axis=1, keepdims=True)
    )
    logit_grad = (LOGIT_SCALE * (grad_combine + grad_dispatch)).astype(jnp.bfloat16)
    images_grad = (
        jnp.einsum("bte,bed->btd", dispatch_low, returned[1], preferred_element_type=jnp.float32)
        + jnp.einsum("bte,de->btd", logit_grad, router_low, preferred_element_type=jnp.float32)
    ).astype(jnp.bfloat16)
    hat_part = jnp.einsum("btd,bte->de", images, logit_grad, preferred_element_type=jnp.float32)
    moment_part = jnp.sum(router_low.astype(jnp.float32) * hat_part, axis=0)
    packed = jnp.concatenate(
        (
            hat_part.reshape((devices,) + router.shape),
            jnp.broadcast_to(moment_part, (devices, 1) + moment_part.shape),
        ),
        axis=1,
    )
    summed = jnp.sum(
        lax.all_to_all(packed, ("exp", "rep"), split_axis=0, concat_axis=0, tiled=True), axis=0
    )
    hat_rows = summed[:-1]
    moment = summed[-1]
    own_hat = router * inv_norm
    router_grad = (hat_rows - own_hat * moment) * inv_norm
    return (images_grad, grad_in[None], grad_out[None], router_grad)


def solution(mesh):
    in_specs = (
        P(("exp", "rep"), None, None),
        P(("exp", "rep"), None),
        P(("exp", "rep"), None, None),
        P(("exp", "rep"), None, None),
        P(("exp", "rep"), None, None),
    )
    out_specs = (
        P(("exp", "rep"), None, None),
        P(("exp", "rep"), None, None),
        P(("exp", "rep"), None, None),
        P(("exp", "rep"), None),
    )
    return jax.shard_map(
        per_device, mesh=mesh, in_specs=in_specs, out_specs=out_specs, check_vma=False
    )
```

```python
import functools

import jax
import jax.numpy as jnp
from jax import lax
from jax.experimental import pallas as pl
from jax.experimental.pallas import tpu as pltpu
from jax.sharding import PartitionSpec as P

LOGIT_SCALE = 2.0
EPS = 1e-06
SQRT_HALF = 0.7071067811865476
INV_ROOT = 0.3989422804014327
LANES = 128
MESH = pl.DeviceIdType.MESH
NN = (((1,), (0,)), ((), ()))
NT = (((1,), (1,)), ((), ()))
TN = (((0,), (0,)), ((), ()))
ROUTER, ROWS, GRADS, OUTS, DXS, HAT, MOMENT = range(7)


def mm(left_side, right_side, dims=NN):
    return lax.dot_general(left_side, right_side, dims, preferred_element_type=jnp.float32)


def gelu_parts(pre_value):
    cumulative = 0.5 * (1.0 + lax.erf(pre_value * SQRT_HALF))
    gelu_slope = cumulative + pre_value * jnp.exp(-0.5 * pre_value * pre_value) * INV_ROOT
    return (pre_value * cumulative, gelu_slope)


def layer_kernel(
    n, rep, tile,
    images_hbm, grad_hbm, w_in_hbm, w_out_hbm, router_ref,
    rows_ref, grads_ref, hidden_ref, pre_grad_ref, left_ref, right_ref, router_grad_ref,
    images, out_grad, w_in, w_out,
    router_all, unpacked, low_packed,
    dispatch, combine, slope, stage,
    sent_a, sent_b, sent_c, sent_d, got_a, got_b, got_c, got_d,
    hat_sent, hat_got, moment_sent, moment_got,
    load_sems, send_sems, recv_sems,
):
    local, tokens, width = images.shape
    slots = n
    chunks = width // LANES
    block = local * chunks
    pack = LANES // slots
    part = router_ref.shape[0] // pack
    hidden_width = w_in.shape[1]
    me = lax.axis_index("exp") * rep + lax.axis_index("rep")

    loads = []
    for i, (source, target) in enumerate(
        ((images_hbm, images), (grad_hbm, out_grad), (w_in_hbm.at[0], w_in), (w_out_hbm.at[0], w_out))
    ):
        loads.append(pltpu.make_async_copy(source, target, load_sems.at[i]))
        loads[-1].start()

    def place(k):
        other = lax.rem(me + k, n)
        return other, (other // rep, lax.rem(other, rep))

    barrier = pltpu.get_barrier_semaphore()

    def greet(k, carry):
        pl.semaphore_signal(barrier, inc=1, device_id=place(k)[1], device_id_type=MESH)
        return carry

    lax.fori_loop(1, n, greet, 0)

    def exchange(phase, size, source, target, whole_source=False):
        def send(k, carry):
            other, where = place(k)
            if whole_source:
                taken = source
            else:
                taken = source.at[pl.ds(pl.multiple_of(other * size, size), size)]
            pltpu.make_async_remote_copy(
                src_ref=taken,
                dst_ref=target.at[pl.ds(pl.multiple_of(me * size, size), size)],
                send_sem=send_sems.at[phase],
                recv_sem=recv_sems.at[phase],
                device_id=where,
                device_id_type=MESH,
            ).start()
            return carry

        lax.fori_loop(1, n, send, 0)

    def settle(sems, phase, size, target):
        span = target.at[pl.ds(0, (n - 1) * size)]
        pltpu.make_async_copy(span, span, sems.at[phase]).wait()

    own_parts = [router_ref[j * part : (j + 1) * part, :] for j in range(pack)]
    own_packed = own_parts[0] if pack == 1 else jnp.concatenate(own_parts, axis=1)
    own_router = pl.ds(pl.multiple_of(me * part, part), part)
    own_block = pl.ds(pl.multiple_of(me * block, block), block)
    router_all[own_router, :] = own_packed
    pl.semaphore_wait(barrier, n - 1)

    def send_router(k, carry):
        pltpu.make_async_remote_copy(
            src_ref=router_all.at[own_router],
            dst_ref=router_all.at[own_router],
            send_sem=send_sems.at[ROUTER],
            recv_sem=recv_sems.at[ROUTER],
            device_id=place(k)[1],
            device_id_type=MESH,
        ).start()
        return carry

    lax.fori_loop(1, n, send_router, 0)

    def group_sum(line):
        total = line
        for j in range(1, pack):
            total = total + pltpu.roll(line, j * slots, 1)
        return total

    settle(recv_sems, ROUTER, part, router_all)
    router_values = router_all[...]
    norm = group_sum(jnp.broadcast_to(jnp.sum(router_values * router_values, axis=0, keepdims=True), (8, LANES)))
    inv_norm = lax.rsqrt(norm + EPS)[0:1, :]
    low = (router_values * inv_norm).astype(jnp.bfloat16).astype(jnp.float32)
    low_packed[...] = low
    for j in range(pack):
        turned = low if j == 0 else pltpu.roll(low, LANES - j * slots, 1)
        unpacked[:, j * part : (j + 1) * part, :] = turned.reshape(n, part, LANES)
    router_low = jnp.transpose(unpacked[...].reshape(width, LANES))[:slots].astype(jnp.bfloat16)
    for b in range(local):
        right_ref[b, slots:, :] = router_low

    loads[0].wait()
    for b in range(local):
        logits = LOGIT_SCALE * mm(router_low, images[b], NT)
        powers = jnp.exp(logits - jnp.max(logits, axis=1, keepdims=True))
        soft = powers / jnp.sum(powers, axis=1, keepdims=True)
        dispatch[b] = soft
        soft_low = soft.astype(jnp.bfloat16)
        left_ref[b, :slots, :] = soft_low
        powers = jnp.exp(logits - jnp.max(logits, axis=0, keepdims=True))
        combine[b] = powers / jnp.sum(powers, axis=0, keepdims=True)
        slot_in = mm(soft_low, images[b])
        for c in range(chunks):
            stage[pl.ds(b * chunks + c, n, stride=block), :] = slot_in[:, c * LANES : (c + 1) * LANES]
    sent_a[...] = stage[...].astype(jnp.bfloat16)
    got_a[own_block, :] = sent_a[own_block, :]
    exchange(ROWS, block, sent_a, got_a)

    loads[1].wait()
    for b in range(local):
        slot_grad = mm(combine[b].astype(jnp.bfloat16), out_grad[b])
        for c in range(chunks):
            stage[pl.ds(b * chunks + c, n, stride=block), :] = slot_grad[:, c * LANES : (c + 1) * LANES]
    sent_b[...] = stage[...].astype(jnp.bfloat16)
    got_b[own_block, :] = sent_b[own_block, :]
    exchange(GRADS, block, sent_b, got_b)

    def gather_rows(source, target):
        stage[...] = source[...].astype(jnp.float32)
        for c in range(chunks):
            target[:, c * LANES : (c + 1) * LANES] = stage[pl.ds(c, n * local, stride=chunks), :].astype(jnp.bfloat16)

    def spread_rows(values, target, own):
        for c in range(chunks):
            stage[pl.ds(c, n * local, stride=chunks), :] = values[:, c * LANES : (c + 1) * LANES]
        target[...] = stage[...].astype(jnp.bfloat16)
        own[own_block, :] = target[own_block, :]

    loads[2].wait()
    loads[3].wait()
    settle(recv_sems, ROWS, block, got_a)
    gather_rows(got_a, rows_ref)
    slot_rows = rows_ref[...]
    total = None
    for start in range(0, hidden_width, tile):
        span = slice(start, start + tile)
        activated, gelu_slope = gelu_parts(mm(slot_rows, w_in[:, span]))
        hidden = activated.astype(jnp.bfloat16)
        hidden_ref[:, span] = hidden
        slope[:, span] = gelu_slope
        term = mm(hidden, w_out[span, :])
        total = term if total is None else total + term
    spread_rows(total, sent_c, got_c)
    exchange(OUTS, block, sent_c, got_c)

    settle(recv_sems, GRADS, block, got_b)
    gather_rows(got_b, grads_ref)
    slot_grads = grads_ref[...]
    total = None
    for start in range(0, hidden_width, tile):
        span = slice(start, start + tile)
        pre_grad = (mm(slot_grads, w_out[span, :], NT) * slope[:, span]).astype(jnp.bfloat16)
        pre_grad_ref[:, span] = pre_grad
        term = mm(pre_grad, w_in[:, span], NT)
        total = term if total is None else total + term
    spread_rows(total, sent_d, got_d)
    exchange(DXS, block, sent_d, got_d)

    def slot_values(b):
        pieces = [stage[pl.ds(b * chunks + c, n, stride=block), :] for c in range(chunks)]
        return jnp.concatenate(pieces, axis=1).astype(jnp.bfloat16)

    settle(recv_sems, OUTS, block, got_c)
    stage[...] = got_c[...].astype(jnp.float32)
    for b in range(local):
        combine_grad = mm(slot_values(b), out_grad[b], NT)
        soft = combine[b]
        combine[b] = soft * (combine_grad - jnp.sum(soft * combine_grad, axis=0, keepdims=True))

    settle(recv_sems, DXS, block, got_d)
    stage[...] = got_d[...].astype(jnp.float32)
    hat = None
    for b in range(local):
        slot_dx = slot_values(b)
        right_ref[b, :slots, :] = slot_dx
        dispatch_grad = mm(slot_dx, images[b], NT)
        soft = dispatch[b]
        grad_dispatch = soft * (dispatch_grad - jnp.sum(soft * dispatch_grad, axis=1, keepdims=True))
        logit_grad = (LOGIT_SCALE * (combine[b] + grad_dispatch)).astype(jnp.bfloat16)
        left_ref[b, slots:, :] = logit_grad
        term = mm(logit_grad, images[b])
        hat = term if hat is None else hat + term
    if slots < LANES:
        hat = jnp.concatenate((hat, jnp.zeros((LANES - slots, width), jnp.float32)), axis=0)
    unpacked[...] = jnp.transpose(hat).reshape(n, pack * part, LANES)
    packed = unpacked[:, 0:part, :].reshape(n * part, LANES)
    for j in range(1, pack):
        packed = packed + pltpu.roll(
            unpacked[:, j * part : (j + 1) * part, :].reshape(n * part, LANES), j * slots, 1
        )
    hat_sent[...] = packed
    hat_got[own_router, :] = hat_sent[own_router, :]
    exchange(HAT, part, hat_sent, hat_got)
    moment = group_sum(jnp.broadcast_to(jnp.sum(packed * low_packed[...], axis=0, keepdims=True), (8, LANES)))
    moment_sent[...] = moment[0:1, :].reshape(1, 1, LANES)
    moment_got[pl.ds(me, 1)] = moment_sent[...]
    exchange(MOMENT, 1, moment_sent, moment_got, whole_source=True)

    settle(recv_sems, HAT, part, hat_got)
    settle(recv_sems, MOMENT, 1, moment_got)
    hat_rows = jnp.sum(hat_got[...].reshape(n, part, LANES), axis=0)
    moment_whole = jnp.sum(moment_got[...], axis=0)
    own_hat = router_all[own_router, :] * inv_norm
    result = (hat_rows - own_hat * moment_whole) * inv_norm
    for j in range(pack):
        turned = result if j == 0 else pltpu.roll(result, LANES - j * slots, 1)
        router_grad_ref[j * part : (j + 1) * part, :] = turned[:, :slots]

    settle(send_sems, ROUTER, part, router_all)
    settle(send_sems, ROWS, block, sent_a)
    settle(send_sems, GRADS, block, sent_b)
    settle(send_sems, OUTS, block, sent_c)
    settle(send_sems, DXS, block, sent_d)
    settle(send_sems, HAT, part, hat_sent)
    settle(send_sems, MOMENT, 1, moment_got)


def weights_kernel(
    rows_ref, grads_ref, hidden_ref, pre_grad_ref, left_ref, right_ref,
    images_grad_ref, grad_in_ref, grad_out_ref,
):
    grad_in_ref[0] = mm(rows_ref[...], pre_grad_ref[...], TN).astype(jnp.bfloat16)
    grad_out_ref[0] = mm(hidden_ref[...], grads_ref[...], TN).astype(jnp.bfloat16)
    images_grad_ref[0] = mm(left_ref[0], right_ref[0], TN).astype(jnp.bfloat16)


def per_device(n, rep, images, router, w_in, w_out, out_grad):
    local, tokens, width = images.shape
    hidden_width = w_in.shape[2]
    slots = router.shape[1]
    images_all = local * n
    chunks = width // LANES
    block = local * chunks
    part = router.shape[0] * slots // LANES
    low, full = jnp.bfloat16, jnp.float32
    vmem = pl.BlockSpec(memory_space=pltpu.VMEM)
    anywhere = pl.BlockSpec(memory_space=pl.ANY)
    slot_rows, slot_grads, hidden, pre_grad, left, right, router_grad = pl.pallas_call(
        functools.partial(layer_kernel, n, rep, 640),
        out_shape=(
            jax.ShapeDtypeStruct((images_all, width), low),
            jax.ShapeDtypeStruct((images_all, width), low),
            jax.ShapeDtypeStruct((images_all, hidden_width), low),
            jax.ShapeDtypeStruct((images_all, hidden_width), low),
            jax.ShapeDtypeStruct((local, 2 * slots, tokens), low),
            jax.ShapeDtypeStruct((local, 2 * slots, width), low),
            jax.ShapeDtypeStruct(router.shape, full),
        ),
        in_specs=[anywhere] * 4 + [vmem],
        out_specs=(vmem,) * 7,
        scratch_shapes=[
            pltpu.VMEM((local, tokens, width), low),
            pltpu.VMEM((local, tokens, width), low),
            pltpu.VMEM((width, hidden_width), low),
            pltpu.VMEM((hidden_width, width), low),
            pltpu.VMEM((n * part, LANES), full),
            pltpu.VMEM((n, router.shape[0], LANES), full),
            pltpu.VMEM((n * part, LANES), full),
            pltpu.VMEM((local, slots, tokens), full),
            pltpu.VMEM((local, slots, tokens), full),
            pltpu.VMEM((images_all, hidden_width), full),
            pltpu.VMEM((n * block, LANES), full),
        ]
        + [pltpu.VMEM((n * block, LANES), low)] * 8
        + [
            pltpu.VMEM((n * part, LANES), full),
            pltpu.VMEM((n * part, LANES), full),
            pltpu.VMEM((1, 1, LANES), full),
            pltpu.VMEM((n, 1, LANES), full),
            pltpu.SemaphoreType.DMA((4,)),
            pltpu.SemaphoreType.DMA((7,)),
            pltpu.SemaphoreType.DMA((7,)),
        ],
        compiler_params=pltpu.CompilerParams(
            collective_id=0, has_side_effects=True, vmem_limit_bytes=48 * 1024 * 1024
        ),
        name="layer",
    )(images, out_grad, w_in, w_out, router)

    steps = 4
    tile = hidden_width // steps
    per_image = steps // local
    token_tile = tokens // per_image
    fixed = lambda i: (0, 0)
    images_grad, grad_in, grad_out = pl.pallas_call(
        weights_kernel,
        grid=(steps,),
        out_shape=(
            jax.ShapeDtypeStruct(images.shape, low),
            jax.ShapeDtypeStruct((1, width, hidden_width), low),
            jax.ShapeDtypeStruct((1, hidden_width, width), low),
        ),
        in_specs=[
            pl.BlockSpec((images_all, width), fixed),
            pl.BlockSpec((images_all, width), fixed),
            pl.BlockSpec((images_all, tile), lambda i: (0, i)),
            pl.BlockSpec((images_all, tile), lambda i: (0, i)),
            pl.BlockSpec((1, 2 * slots, token_tile), lambda i: (i // per_image, 0, i % per_image)),
            pl.BlockSpec((1, 2 * slots, width), lambda i: (i // per_image, 0, 0)),
        ],
        out_specs=(
            pl.BlockSpec((1, token_tile, width), lambda i: (i // per_image, i % per_image, 0)),
            pl.BlockSpec((1, width, tile), lambda i: (0, 0, i)),
            pl.BlockSpec((1, tile, width), lambda i: (0, i, 0)),
        ),
        compiler_params=pltpu.CompilerParams(vmem_limit_bytes=32 * 1024 * 1024),
        name="weights",
    )(slot_rows, slot_grads, hidden, pre_grad, left, right)
    return (images_grad, grad_in, grad_out, router_grad)


def solution(mesh):
    in_specs = (
        P(("exp", "rep"), None, None),
        P(("exp", "rep"), None),
        P(("exp", "rep"), None, None),
        P(("exp", "rep"), None, None),
        P(("exp", "rep"), None, None),
    )
    out_specs = (
        P(("exp", "rep"), None, None),
        P(("exp", "rep"), None, None),
        P(("exp", "rep"), None, None),
        P(("exp", "rep"), None),
    )
    rep = mesh.shape["rep"]
    n = mesh.shape["exp"] * rep
    return jax.shard_map(
        functools.partial(per_device, n, rep),
        mesh=mesh, in_specs=in_specs, out_specs=out_specs, check_vma=False,
    )
```

```python
import functools

import jax
import jax.numpy as jnp
from jax import lax
from jax.experimental import pallas as pl
from jax.experimental.pallas import tpu as pltpu
from jax.sharding import PartitionSpec as P

LOGIT_SCALE = 2.0
EPS = 1e-06
SQRT_HALF = 0.7071067811865476
INV_ROOT = 0.3989422804014327
LANES = 128
MESH = pl.DeviceIdType.MESH
NN = (((1,), (0,)), ((), ()))
NT = (((1,), (1,)), ((), ()))
TN = (((0,), (0,)), ((), ()))
ROUTER, ROWS, GRADS, OUTS, DXS, HAT, MOMENT = range(7)


def mm(left_side, right_side, dims=NN):
    return lax.dot_general(left_side, right_side, dims, preferred_element_type=jnp.float32)


def gelu_parts(pre_value):
    cumulative = 0.5 * (1.0 + lax.erf(pre_value * SQRT_HALF))
    gelu_slope = cumulative + pre_value * jnp.exp(-0.5 * pre_value * pre_value) * INV_ROOT
    return (pre_value * cumulative, gelu_slope)


def layer_kernel(
    n, rep, tile,
    images_hbm, grad_hbm, w_in_hbm, w_out_hbm, router_hbm,
    images_grad_ref, grad_in_ref, grad_out_ref, router_grad_ref,
    rows_ref, grads_ref, hidden_ref, pre_grad_ref, left_ref, right_ref,
    router_ref, images, out_grad, w_in, w_out,
    router_all, unpacked, low_packed,
    dispatch, combine, slope, stage,
    sent_a, sent_b, sent_c, sent_d, got_a, got_b, got_c, got_d,
    hat_sent, hat_got, moment_sent, moment_got,
    load_sems, send_sems, recv_sems,
):
    local, tokens, width = images.shape
    slots = n
    chunks = width // LANES
    block = local * chunks
    pack = LANES // slots
    part = router_ref.shape[0] // pack
    hidden_width = w_in.shape[1]
    me = lax.axis_index("exp") * rep + lax.axis_index("rep")

    def load(i, source, target, pieces):
        rows = target.shape[0] // pieces
        for k in range(pieces):
            span = pl.ds(k * rows, rows)
            pltpu.make_async_copy(source.at[span], target.at[span], load_sems.at[i, k]).start()

    def loaded(i, source, target, pieces):
        rows = target.shape[0] // pieces
        for k in range(pieces):
            span = pl.ds(k * rows, rows)
            pltpu.make_async_copy(source.at[span], target.at[span], load_sems.at[i, k]).wait()

    loads = (
        (4, router_hbm, router_ref, 1),
        (0, images_hbm, images, local),
        (1, grad_hbm, out_grad, local),
        (2, w_in_hbm.at[0], w_in, 4),
        (3, w_out_hbm.at[0], w_out, 4),
    )
    for one in loads:
        load(*one)

    def place(k):
        other = lax.rem(me + k, n)
        return other, (lax.div(other, rep), lax.rem(other, rep))

    barrier = pltpu.get_barrier_semaphore()

    def greet(k, carry):
        pl.semaphore_signal(barrier, inc=1, device_id=place(k)[1], device_id_type=MESH)
        return carry

    lax.fori_loop(1, n, greet, 0)

    def exchange(phase, size, source, target, whole_source=False):
        def send(k, carry):
            other, where = place(k)
            if whole_source:
                taken = source
            else:
                taken = source.at[pl.ds(pl.multiple_of(other * size, size), size)]
            pltpu.make_async_remote_copy(
                src_ref=taken,
                dst_ref=target.at[pl.ds(pl.multiple_of(me * size, size), size)],
                send_sem=send_sems.at[phase],
                recv_sem=recv_sems.at[phase],
                device_id=where,
                device_id_type=MESH,
            ).start()
            return carry

        lax.fori_loop(1, n, send, 0)

    def settle(sems, phase, size, target):
        span = target.at[pl.ds(0, (n - 1) * size)]
        pltpu.make_async_copy(span, span, sems.at[phase]).wait()

    loaded(*loads[0])
    own_parts = [router_ref[j * part : (j + 1) * part, :] for j in range(pack)]
    own_packed = own_parts[0] if pack == 1 else jnp.concatenate(own_parts, axis=1)
    own_router = pl.ds(pl.multiple_of(me * part, part), part)
    own_block = pl.ds(pl.multiple_of(me * block, block), block)
    router_all[own_router, :] = own_packed
    pl.semaphore_wait(barrier, n - 1)

    def send_router(k, carry):
        pltpu.make_async_remote_copy(
            src_ref=router_all.at[own_router],
            dst_ref=router_all.at[own_router],
            send_sem=send_sems.at[ROUTER],
            recv_sem=recv_sems.at[ROUTER],
            device_id=place(k)[1],
            device_id_type=MESH,
        ).start()
        return carry

    lax.fori_loop(1, n, send_router, 0)

    def group_sum(line):
        total = line
        for j in range(1, pack):
            total = total + pltpu.roll(line, j * slots, 1)
        return total

    settle(recv_sems, ROUTER, part, router_all)
    router_values = router_all[...]
    norm = group_sum(jnp.broadcast_to(jnp.sum(router_values * router_values, axis=0, keepdims=True), (8, LANES)))
    inv_norm = lax.rsqrt(norm + EPS)[0:1, :]
    low = (router_values * inv_norm).astype(jnp.bfloat16).astype(jnp.float32)
    low_packed[...] = low
    for j in range(pack):
        turned = low if j == 0 else pltpu.roll(low, LANES - j * slots, 1)
        unpacked[:, j * part : (j + 1) * part, :] = turned.reshape(n, part, LANES)
    router_low = jnp.transpose(unpacked[...].reshape(width, LANES))[:slots].astype(jnp.bfloat16)
    for b in range(local):
        right_ref[b, slots:, :] = router_low

    loaded(*loads[1])
    for b in range(local):
        logits = LOGIT_SCALE * mm(router_low, images[b], NT)
        powers = jnp.exp(logits - jnp.max(logits, axis=1, keepdims=True))
        soft = powers / jnp.sum(powers, axis=1, keepdims=True)
        dispatch[b] = soft
        soft_low = soft.astype(jnp.bfloat16)
        left_ref[b, :slots, :] = soft_low
        powers = jnp.exp(logits - jnp.max(logits, axis=0, keepdims=True))
        combine[b] = powers / jnp.sum(powers, axis=0, keepdims=True)
        slot_in = mm(soft_low, images[b])
        for c in range(chunks):
            stage[pl.ds(b * chunks + c, n, stride=block), :] = slot_in[:, c * LANES : (c + 1) * LANES]
    sent_a[...] = stage[...].astype(jnp.bfloat16)
    got_a[own_block, :] = sent_a[own_block, :]
    exchange(ROWS, block, sent_a, got_a)

    loaded(*loads[2])
    for b in range(local):
        slot_grad = mm(combine[b].astype(jnp.bfloat16), out_grad[b])
        for c in range(chunks):
            stage[pl.ds(b * chunks + c, n, stride=block), :] = slot_grad[:, c * LANES : (c + 1) * LANES]
    sent_b[...] = stage[...].astype(jnp.bfloat16)
    got_b[own_block, :] = sent_b[own_block, :]
    exchange(GRADS, block, sent_b, got_b)

    def gather_rows(source, target):
        stage[...] = source[...].astype(jnp.float32)
        for c in range(chunks):
            target[:, c * LANES : (c + 1) * LANES] = stage[pl.ds(c, n * local, stride=chunks), :].astype(jnp.bfloat16)

    def spread_rows(values, target, own):
        for c in range(chunks):
            stage[pl.ds(c, n * local, stride=chunks), :] = values[:, c * LANES : (c + 1) * LANES]
        target[...] = stage[...].astype(jnp.bfloat16)
        own[own_block, :] = target[own_block, :]

    loaded(*loads[3])
    loaded(*loads[4])
    settle(recv_sems, ROWS, block, got_a)
    gather_rows(got_a, rows_ref)
    slot_rows = rows_ref[...]
    total = None
    for start in range(0, hidden_width, tile):
        span = slice(start, start + tile)
        activated, gelu_slope = gelu_parts(mm(slot_rows, w_in[:, span]))
        hidden = activated.astype(jnp.bfloat16)
        hidden_ref[:, span] = hidden
        slope[:, span] = gelu_slope
        term = mm(hidden, w_out[span, :])
        total = term if total is None else total + term
    spread_rows(total, sent_c, got_c)
    exchange(OUTS, block, sent_c, got_c)

    settle(recv_sems, GRADS, block, got_b)
    gather_rows(got_b, grads_ref)
    slot_grads = grads_ref[...]
    total = None
    for start in range(0, hidden_width, tile):
        span = slice(start, start + tile)
        pre_grad = (mm(slot_grads, w_out[span, :], NT) * slope[:, span]).astype(jnp.bfloat16)
        pre_grad_ref[:, span] = pre_grad
        term = mm(pre_grad, w_in[:, span], NT)
        total = term if total is None else total + term
    spread_rows(total, sent_d, got_d)
    exchange(DXS, block, sent_d, got_d)

    for start in range(0, hidden_width, tile):
        span = slice(start, start + tile)
        grad_out_ref[span, :] = mm(hidden_ref[:, span], slot_grads, TN).astype(jnp.bfloat16)

    def slot_values(b):
        pieces = [stage[pl.ds(b * chunks + c, n, stride=block), :] for c in range(chunks)]
        return jnp.concatenate(pieces, axis=1).astype(jnp.bfloat16)

    settle(recv_sems, OUTS, block, got_c)
    stage[...] = got_c[...].astype(jnp.float32)
    for b in range(local):
        combine_grad = mm(slot_values(b), out_grad[b], NT)
        soft = combine[b]
        combine[b] = soft * (combine_grad - jnp.sum(soft * combine_grad, axis=0, keepdims=True))

    settle(recv_sems, DXS, block, got_d)
    stage[...] = got_d[...].astype(jnp.float32)
    hat = None
    for b in range(local):
        slot_dx = slot_values(b)
        right_ref[b, :slots, :] = slot_dx
        dispatch_grad = mm(slot_dx, images[b], NT)
        soft = dispatch[b]
        grad_dispatch = soft * (dispatch_grad - jnp.sum(soft * dispatch_grad, axis=1, keepdims=True))
        logit_grad = (LOGIT_SCALE * (combine[b] + grad_dispatch)).astype(jnp.bfloat16)
        left_ref[b, slots:, :] = logit_grad
        term = mm(logit_grad, images[b])
        hat = term if hat is None else hat + term
    if slots < LANES:
        hat = jnp.concatenate((hat, jnp.zeros((LANES - slots, width), jnp.float32)), axis=0)
    unpacked[...] = jnp.transpose(hat).reshape(n, pack * part, LANES)
    packed = unpacked[:, 0:part, :].reshape(n * part, LANES)
    for j in range(1, pack):
        packed = packed + pltpu.roll(
            unpacked[:, j * part : (j + 1) * part, :].reshape(n * part, LANES), j * slots, 1
        )
    hat_sent[...] = packed
    hat_got[own_router, :] = hat_sent[own_router, :]
    exchange(HAT, part, hat_sent, hat_got)
    moment = group_sum(jnp.broadcast_to(jnp.sum(packed * low_packed[...], axis=0, keepdims=True), (8, LANES)))
    moment_sent[...] = moment[0:1, :].reshape(1, 1, LANES)
    moment_got[pl.ds(me, 1)] = moment_sent[...]
    exchange(MOMENT, 1, moment_sent, moment_got, whole_source=True)

    for b in range(local):
        images_grad_ref[b] = mm(left_ref[b], right_ref[b], TN).astype(jnp.bfloat16)
    rows_turned = jnp.transpose(rows_ref[...].astype(jnp.float32)).astype(jnp.bfloat16)
    for start in range(0, hidden_width, tile):
        span = slice(start, start + tile)
        grad_in_ref[:, span] = mm(rows_turned, pre_grad_ref[:, span]).astype(jnp.bfloat16)

    settle(recv_sems, HAT, part, hat_got)
    settle(recv_sems, MOMENT, 1, moment_got)
    hat_rows = jnp.sum(hat_got[...].reshape(n, part, LANES), axis=0)
    moment_whole = jnp.sum(moment_got[...], axis=0)
    own_hat = router_all[own_router, :] * inv_norm
    result = (hat_rows - own_hat * moment_whole) * inv_norm
    for j in range(pack):
        turned = result if j == 0 else pltpu.roll(result, LANES - j * slots, 1)
        router_grad_ref[j * part : (j + 1) * part, :] = turned[:, :slots]

    settle(send_sems, ROUTER, part, router_all)
    settle(send_sems, ROWS, block, sent_a)
    settle(send_sems, GRADS, block, sent_b)
    settle(send_sems, OUTS, block, sent_c)
    settle(send_sems, DXS, block, sent_d)
    settle(send_sems, HAT, part, hat_sent)
    settle(send_sems, MOMENT, 1, moment_got)


def drain_kernel(pieces, *refs):
    count = len(pieces)
    sources, targets, sems = refs[:count], refs[count : 2 * count], refs[-1]
    copies = []
    for source, target, cuts in zip(sources, targets, pieces):
        rows = source.shape[0] // cuts
        for k in range(cuts):
            span = pl.ds(k * rows, rows)
            copies.append(pltpu.make_async_copy(source.at[span], target.at[span], sems.at[len(copies)]))
            copies[-1].start()
    for copy in copies:
        copy.wait()


def per_device(n, rep, images, router, w_in, w_out, out_grad):
    local, tokens, width = images.shape
    hidden_width = w_in.shape[2]
    slots = router.shape[1]
    images_all = local * n
    chunks = width // LANES
    block = local * chunks
    part = router.shape[0] * slots // LANES
    low, full = jnp.bfloat16, jnp.float32
    vmem = pl.BlockSpec(memory_space=pltpu.VMEM)
    anywhere = pl.BlockSpec(memory_space=pl.ANY)
    in_hbm = pl.BlockSpec(memory_space=pltpu.HBM)
    results = (
        jax.ShapeDtypeStruct(images.shape, low),
        jax.ShapeDtypeStruct(w_in.shape[1:], low),
        jax.ShapeDtypeStruct(w_out.shape[1:], low),
        jax.ShapeDtypeStruct(router.shape, full),
    )
    made = pl.pallas_call(
        functools.partial(layer_kernel, n, rep, 640),
        out_shape=results,
        in_specs=[in_hbm] * 5,
        out_specs=(vmem,) * 4,
        scratch_shapes=[
            pltpu.VMEM((images_all, width), low),
            pltpu.VMEM((images_all, width), low),
            pltpu.VMEM((images_all, hidden_width), low),
            pltpu.VMEM((images_all, hidden_width), low),
            pltpu.VMEM((local, 2 * slots, tokens), low),
            pltpu.VMEM((local, 2 * slots, width), low),
            pltpu.VMEM(router.shape, full),
            pltpu.VMEM((local, tokens, width), low),
            pltpu.VMEM((local, tokens, width), low),
            pltpu.VMEM((width, hidden_width), low),
            pltpu.VMEM((hidden_width, width), low),
            pltpu.VMEM((n * part, LANES), full),
            pltpu.VMEM((n, router.shape[0], LANES), full),
            pltpu.VMEM((n * part, LANES), full),
            pltpu.VMEM((local, slots, tokens), full),
            pltpu.VMEM((local, slots, tokens), full),
            pltpu.VMEM((images_all, hidden_width), full),
            pltpu.VMEM((n * block, LANES), full),
        ]
        + [pltpu.VMEM((n * block, LANES), low)] * 8
        + [
            pltpu.VMEM((n * part, LANES), full),
            pltpu.VMEM((n * part, LANES), full),
            pltpu.VMEM((1, 1, LANES), full),
            pltpu.VMEM((n, 1, LANES), full),
            pltpu.SemaphoreType.DMA((5, 4)),
            pltpu.SemaphoreType.DMA((7,)),
            pltpu.SemaphoreType.DMA((7,)),
        ],
        compiler_params=pltpu.CompilerParams(
            collective_id=0, has_side_effects=True, vmem_limit_bytes=40 * 1024 * 1024
        ),
        name="layer",
    )(*(pltpu.with_memory_space_constraint(x, pltpu.HBM) for x in (images, out_grad, w_in, w_out, router)))

    pieces = (local, 8, 8, 1)
    images_grad, grad_in, grad_out, router_grad = pl.pallas_call(
        functools.partial(drain_kernel, pieces),
        out_shape=results,
        in_specs=[vmem] * 4,
        out_specs=(in_hbm,) * 4,
        scratch_shapes=[pltpu.SemaphoreType.DMA((sum(pieces),))],
        name="drain",
    )(*made)
    return (images_grad, grad_in[None], grad_out[None], router_grad)


def solution(mesh):
    in_specs = (
        P(("exp", "rep"), None, None),
        P(("exp", "rep"), None),
        P(("exp", "rep"), None, None),
        P(("exp", "rep"), None, None),
        P(("exp", "rep"), None, None),
    )
    out_specs = (
        P(("exp", "rep"), None, None),
        P(("exp", "rep"), None, None),
        P(("exp", "rep"), None, None),
        P(("exp", "rep"), None),
    )
    rep = mesh.shape["rep"]
    n = mesh.shape["exp"] * rep
    return jax.shard_map(
        functools.partial(per_device, n, rep),
        mesh=mesh, in_specs=in_specs, out_specs=out_specs, check_vma=False,
    )
```

```python
import functools

import jax
import jax.numpy as jnp
from jax import lax
from jax.experimental import pallas as pl
from jax.experimental.pallas import tpu as pltpu
from jax.sharding import PartitionSpec as P

LOGIT_SCALE = 2.0
EPS = 1e-06
SQRT_HALF = 0.7071067811865476
INV_ROOT = 0.3989422804014327
LANES = 128
LOGICAL = pl.DeviceIdType.LOGICAL
GROUP = 8
NN = (((1,), (0,)), ((), ()))
NT = (((1,), (1,)), ((), ()))
TN = (((0,), (0,)), ((), ()))
ROUTER, ROWS, GRADS, OUTS, DXS, HAT, MOMENT = range(7)


def mm(left_side, right_side, dims=NN):
    return lax.dot_general(left_side, right_side, dims, preferred_element_type=jnp.float32)


def gelu_parts(pre_value):
    cumulative = 0.5 * (1.0 + lax.erf(pre_value * SQRT_HALF))
    gelu_slope = cumulative + pre_value * jnp.exp(-0.5 * pre_value * pre_value) * INV_ROOT
    return (pre_value * cumulative, gelu_slope)


def layer_kernel(
    n, rep, tile,
    images_hbm, grad_hbm, w_in_hbm, w_out_hbm, router_hbm,
    images_grad_ref, grad_in_ref, grad_out_ref, router_grad_ref,
    rows_ref, grads_ref, hidden_ref, pre_grad_ref, left_ref, right_ref,
    router_ref, images, out_grad, w_in, w_out,
    router_all, unpacked, low_packed,
    dispatch, combine, slope, stage,
    sent_a, sent_b, sent_c, sent_d, got_a, got_b, got_c, got_d,
    hat_sent, hat_got, moment_sent, moment_got,
    load_sems, send_sems, recv_sems,
):
    local, tokens, width = images.shape
    slots = n
    chunks = width // LANES
    block = local * chunks
    pack = LANES // slots
    part = router_ref.shape[0] // pack
    hidden_width = w_in.shape[1]
    me = lax.axis_index("exp") * rep + lax.axis_index("rep")

    def load(i, source, target, pieces):
        rows = target.shape[0] // pieces
        for k in range(pieces):
            span = pl.ds(k * rows, rows)
            pltpu.make_async_copy(source.at[span], target.at[span], load_sems.at[i, k]).start()

    def loaded(i, source, target, pieces):
        rows = target.shape[0] // pieces
        for k in range(pieces):
            span = pl.ds(k * rows, rows)
            pltpu.make_async_copy(source.at[span], target.at[span], load_sems.at[i, k]).wait()

    loads = (
        (4, router_hbm, router_ref, 1),
        (0, images_hbm, images, local),
        (1, grad_hbm, out_grad, local),
        (2, w_in_hbm.at[0], w_in, 4),
        (3, w_out_hbm.at[0], w_out, 4),
    )
    load(*loads[0])

    def each_other(act):
        def one(base, step):
            half = (step + 1) // 2
            k = n // 2 + (base + half if step % 2 == 0 else -(base + half))
            other = me + k
            act(jnp.where(other >= n, other - n, other))

        def group(g, carry):
            for step in range(GROUP):
                one(g * (GROUP // 2), step)
            return carry

        groups = (n - 1) // GROUP
        lax.fori_loop(0, groups, group, 0)
        for step in range(n - 1 - groups * GROUP):
            one(groups * (GROUP // 2), step)

    barrier = pltpu.get_barrier_semaphore()

    def greet(other):
        pl.semaphore_signal(barrier, inc=1, device_id=other, device_id_type=LOGICAL)

    each_other(greet)
    for one_load in loads[1:]:
        load(*one_load)

    def exchange(phase, size, source, target, whole_source=False):
        def send(other):
            if whole_source:
                taken = source
            else:
                taken = source.at[pl.ds(pl.multiple_of(other * size, size), size)]
            pltpu.make_async_remote_copy(
                src_ref=taken,
                dst_ref=target.at[pl.ds(pl.multiple_of(me * size, size), size)],
                send_sem=send_sems.at[phase],
                recv_sem=recv_sems.at[phase],
                device_id=other,
                device_id_type=LOGICAL,
            ).start()

        each_other(send)

    def settle(sems, phase, size, target):
        span = target.at[pl.ds(0, (n - 1) * size)]
        pltpu.make_async_copy(span, span, sems.at[phase]).wait()

    loaded(*loads[0])
    own_parts = [router_ref[j * part : (j + 1) * part, :] for j in range(pack)]
    own_packed = own_parts[0] if pack == 1 else jnp.concatenate(own_parts, axis=1)
    own_router = pl.ds(pl.multiple_of(me * part, part), part)
    own_block = pl.ds(pl.multiple_of(me * block, block), block)
    router_all[own_router, :] = own_packed
    pl.semaphore_wait(barrier, n - 1)

    def send_router(other):
        pltpu.make_async_remote_copy(
            src_ref=router_all.at[own_router],
            dst_ref=router_all.at[own_router],
            send_sem=send_sems.at[ROUTER],
            recv_sem=recv_sems.at[ROUTER],
            device_id=other,
            device_id_type=LOGICAL,
        ).start()

    each_other(send_router)

    def group_sum(line):
        total = line
        for j in range(1, pack):
            total = total + pltpu.roll(line, j * slots, 1)
        return total

    settle(recv_sems, ROUTER, part, router_all)
    router_values = router_all[...]
    norm = group_sum(jnp.broadcast_to(jnp.sum(router_values * router_values, axis=0, keepdims=True), (8, LANES)))
    inv_norm = lax.rsqrt(norm + EPS)[0:1, :]
    low = (router_values * inv_norm).astype(jnp.bfloat16).astype(jnp.float32)
    low_packed[...] = low
    for j in range(pack):
        turned = low if j == 0 else pltpu.roll(low, LANES - j * slots, 1)
        unpacked[:, j * part : (j + 1) * part, :] = turned.reshape(n, part, LANES)
    router_low = jnp.transpose(unpacked[...].reshape(width, LANES))[:slots].astype(jnp.bfloat16)
    for b in range(local):
        right_ref[b, slots:, :] = router_low

    loaded(*loads[1])
    for b in range(local):
        logits = LOGIT_SCALE * mm(router_low, images[b], NT)
        powers = jnp.exp(logits - jnp.max(logits, axis=1, keepdims=True))
        soft = powers / jnp.sum(powers, axis=1, keepdims=True)
        dispatch[b] = soft
        soft_low = soft.astype(jnp.bfloat16)
        left_ref[b, :slots, :] = soft_low
        powers = jnp.exp(logits - jnp.max(logits, axis=0, keepdims=True))
        combine[b] = powers / jnp.sum(powers, axis=0, keepdims=True)
        slot_in = mm(soft_low, images[b])
        for c in range(chunks):
            stage[pl.ds(b * chunks + c, n, stride=block), :] = slot_in[:, c * LANES : (c + 1) * LANES]
    sent_a[...] = stage[...].astype(jnp.bfloat16)
    got_a[own_block, :] = sent_a[own_block, :]
    exchange(ROWS, block, sent_a, got_a)

    loaded(*loads[2])
    for b in range(local):
        slot_grad = mm(combine[b].astype(jnp.bfloat16), out_grad[b])
        for c in range(chunks):
            stage[pl.ds(b * chunks + c, n, stride=block), :] = slot_grad[:, c * LANES : (c + 1) * LANES]
    sent_b[...] = stage[...].astype(jnp.bfloat16)
    got_b[own_block, :] = sent_b[own_block, :]
    exchange(GRADS, block, sent_b, got_b)

    def gather_rows(source, target):
        stage[...] = source[...].astype(jnp.float32)
        for c in range(chunks):
            target[:, c * LANES : (c + 1) * LANES] = stage[pl.ds(c, n * local, stride=chunks), :].astype(jnp.bfloat16)

    def spread_rows(values, target, own):
        for c in range(chunks):
            stage[pl.ds(c, n * local, stride=chunks), :] = values[:, c * LANES : (c + 1) * LANES]
        target[...] = stage[...].astype(jnp.bfloat16)
        own[own_block, :] = target[own_block, :]

    loaded(*loads[3])
    loaded(*loads[4])
    settle(recv_sems, ROWS, block, got_a)
    gather_rows(got_a, rows_ref)
    slot_rows = rows_ref[...]
    total = None
    for start in range(0, hidden_width, tile):
        span = slice(start, start + tile)
        activated, gelu_slope = gelu_parts(mm(slot_rows, w_in[:, span]))
        hidden = activated.astype(jnp.bfloat16)
        hidden_ref[:, span] = hidden
        slope[:, span] = gelu_slope
        term = mm(hidden, w_out[span, :])
        total = term if total is None else total + term
    spread_rows(total, sent_c, got_c)
    exchange(OUTS, block, sent_c, got_c)

    settle(recv_sems, GRADS, block, got_b)
    gather_rows(got_b, grads_ref)
    slot_grads = grads_ref[...]
    total = None
    for start in range(0, hidden_width, tile):
        span = slice(start, start + tile)
        pre_grad = (mm(slot_grads, w_out[span, :], NT) * slope[:, span]).astype(jnp.bfloat16)
        pre_grad_ref[:, span] = pre_grad
        term = mm(pre_grad, w_in[:, span], NT)
        total = term if total is None else total + term
    spread_rows(total, sent_d, got_d)
    exchange(DXS, block, sent_d, got_d)

    for start in range(0, hidden_width, tile):
        span = slice(start, start + tile)
        grad_out_ref[span, :] = mm(hidden_ref[:, span], slot_grads, TN).astype(jnp.bfloat16)

    def slot_values(b):
        pieces = [stage[pl.ds(b * chunks + c, n, stride=block), :] for c in range(chunks)]
        return jnp.concatenate(pieces, axis=1).astype(jnp.bfloat16)

    settle(recv_sems, OUTS, block, got_c)
    stage[...] = got_c[...].astype(jnp.float32)
    for b in range(local):
        combine_grad = mm(slot_values(b), out_grad[b], NT)
        soft = combine[b]
        combine[b] = soft * (combine_grad - jnp.sum(soft * combine_grad, axis=0, keepdims=True))

    settle(recv_sems, DXS, block, got_d)
    stage[...] = got_d[...].astype(jnp.float32)
    hat = None
    for b in range(local):
        slot_dx = slot_values(b)
        right_ref[b, :slots, :] = slot_dx
        dispatch_grad = mm(slot_dx, images[b], NT)
        soft = dispatch[b]
        grad_dispatch = soft * (dispatch_grad - jnp.sum(soft * dispatch_grad, axis=1, keepdims=True))
        logit_grad = (LOGIT_SCALE * (combine[b] + grad_dispatch)).astype(jnp.bfloat16)
        left_ref[b, slots:, :] = logit_grad
        term = mm(logit_grad, images[b])
        hat = term if hat is None else hat + term
    if slots < LANES:
        hat = jnp.concatenate((hat, jnp.zeros((LANES - slots, width), jnp.float32)), axis=0)
    unpacked[...] = jnp.transpose(hat).reshape(n, pack * part, LANES)
    packed = unpacked[:, 0:part, :].reshape(n * part, LANES)
    for j in range(1, pack):
        packed = packed + pltpu.roll(
            unpacked[:, j * part : (j + 1) * part, :].reshape(n * part, LANES), j * slots, 1
        )
    hat_sent[...] = packed
    hat_got[own_router, :] = hat_sent[own_router, :]
    exchange(HAT, part, hat_sent, hat_got)
    moment = group_sum(jnp.broadcast_to(jnp.sum(packed * low_packed[...], axis=0, keepdims=True), (8, LANES)))
    moment_sent[...] = moment[0:1, :].reshape(1, 1, LANES)
    moment_got[pl.ds(me, 1)] = moment_sent[...]
    exchange(MOMENT, 1, moment_sent, moment_got, whole_source=True)

    for b in range(local):
        images_grad_ref[b] = mm(left_ref[b], right_ref[b], TN).astype(jnp.bfloat16)
    rows_turned = jnp.transpose(rows_ref[...].astype(jnp.float32)).astype(jnp.bfloat16)
    for start in range(0, hidden_width, tile):
        span = slice(start, start + tile)
        grad_in_ref[:, span] = mm(rows_turned, pre_grad_ref[:, span]).astype(jnp.bfloat16)

    settle(recv_sems, HAT, part, hat_got)
    settle(recv_sems, MOMENT, 1, moment_got)
    hat_rows = jnp.sum(hat_got[...].reshape(n, part, LANES), axis=0)
    moment_whole = jnp.sum(moment_got[...], axis=0)
    own_hat = router_all[own_router, :] * inv_norm
    result = (hat_rows - own_hat * moment_whole) * inv_norm
    for j in range(pack):
        turned = result if j == 0 else pltpu.roll(result, LANES - j * slots, 1)
        router_grad_ref[j * part : (j + 1) * part, :] = turned[:, :slots]

    settle(send_sems, ROUTER, part, router_all)
    settle(send_sems, ROWS, block, sent_a)
    settle(send_sems, GRADS, block, sent_b)
    settle(send_sems, OUTS, block, sent_c)
    settle(send_sems, DXS, block, sent_d)
    settle(send_sems, HAT, part, hat_sent)
    settle(send_sems, MOMENT, 1, moment_got)


def drain_kernel(pieces, *refs):
    count = len(pieces)
    sources, targets, sems = refs[:count], refs[count : 2 * count], refs[-1]
    copies = []
    for source, target, cuts in zip(sources, targets, pieces):
        rows = source.shape[0] // cuts
        for k in range(cuts):
            span = pl.ds(k * rows, rows)
            copies.append(pltpu.make_async_copy(source.at[span], target.at[span], sems.at[len(copies)]))
            copies[-1].start()
    for copy in copies:
        copy.wait()


def per_device(n, rep, images, router, w_in, w_out, out_grad):
    local, tokens, width = images.shape
    hidden_width = w_in.shape[2]
    slots = router.shape[1]
    images_all = local * n
    chunks = width // LANES
    block = local * chunks
    part = router.shape[0] * slots // LANES
    low, full = jnp.bfloat16, jnp.float32
    vmem = pl.BlockSpec(memory_space=pltpu.VMEM)
    anywhere = pl.BlockSpec(memory_space=pl.ANY)
    in_hbm = pl.BlockSpec(memory_space=pltpu.HBM)
    results = (
        jax.ShapeDtypeStruct(images.shape, low),
        jax.ShapeDtypeStruct(w_in.shape[1:], low),
        jax.ShapeDtypeStruct(w_out.shape[1:], low),
        jax.ShapeDtypeStruct(router.shape, full),
    )
    made = pl.pallas_call(
        functools.partial(layer_kernel, n, rep, 640),
        out_shape=results,
        in_specs=[in_hbm] * 5,
        out_specs=(vmem,) * 4,
        scratch_shapes=[
            pltpu.VMEM((images_all, width), low),
            pltpu.VMEM((images_all, width), low),
            pltpu.VMEM((images_all, hidden_width), low),
            pltpu.VMEM((images_all, hidden_width), low),
            pltpu.VMEM((local, 2 * slots, tokens), low),
            pltpu.VMEM((local, 2 * slots, width), low),
            pltpu.VMEM(router.shape, full),
            pltpu.VMEM((local, tokens, width), low),
            pltpu.VMEM((local, tokens, width), low),
            pltpu.VMEM((width, hidden_width), low),
            pltpu.VMEM((hidden_width, width), low),
            pltpu.VMEM((n * part, LANES), full),
            pltpu.VMEM((n, router.shape[0], LANES), full),
            pltpu.VMEM((n * part, LANES), full),
            pltpu.VMEM((local, slots, tokens), full),
            pltpu.VMEM((local, slots, tokens), full),
            pltpu.VMEM((images_all, hidden_width), full),
            pltpu.VMEM((n * block, LANES), full),
        ]
        + [pltpu.VMEM((n * block, LANES), low)] * 8
        + [
            pltpu.VMEM((n * part, LANES), full),
            pltpu.VMEM((n * part, LANES), full),
            pltpu.VMEM((1, 1, LANES), full),
            pltpu.VMEM((n, 1, LANES), full),
            pltpu.SemaphoreType.DMA((5, 4)),
            pltpu.SemaphoreType.DMA((7,)),
            pltpu.SemaphoreType.DMA((7,)),
        ],
        compiler_params=pltpu.CompilerParams(
            collective_id=0, has_side_effects=True, vmem_limit_bytes=40 * 1024 * 1024
        ),
        name="layer",
    )(*(pltpu.with_memory_space_constraint(x, pltpu.HBM) for x in (images, out_grad, w_in, w_out, router)))

    pieces = (local, 8, 8, 1)
    images_grad, grad_in, grad_out, router_grad = pl.pallas_call(
        functools.partial(drain_kernel, pieces),
        out_shape=results,
        in_specs=[anywhere] * 4,
        out_specs=(in_hbm,) * 4,
        scratch_shapes=[pltpu.SemaphoreType.DMA((sum(pieces),))],
        compiler_params=pltpu.CompilerParams(vmem_limit_bytes=2 * 1024 * 1024),
        name="drain",
    )(*made)
    return (images_grad, grad_in[None], grad_out[None], router_grad)


def solution(mesh):
    in_specs = (
        P(("exp", "rep"), None, None),
        P(("exp", "rep"), None),
        P(("exp", "rep"), None, None),
        P(("exp", "rep"), None, None),
        P(("exp", "rep"), None, None),
    )
    out_specs = (
        P(("exp", "rep"), None, None),
        P(("exp", "rep"), None, None),
        P(("exp", "rep"), None, None),
        P(("exp", "rep"), None),
    )
    rep = mesh.shape["rep"]
    n = mesh.shape["exp"] * rep
    return jax.shard_map(
        functools.partial(per_device, n, rep),
        mesh=mesh, in_specs=in_specs, out_specs=out_specs, check_vma=False,
    )
```

```python
import functools

import jax
import jax.numpy as jnp
from jax import lax
from jax.experimental import pallas as pl
from jax.experimental.pallas import tpu as pltpu
from jax.sharding import PartitionSpec as P

LOGIT_SCALE = 2.0
EPS = 1e-06
SQRT_HALF = 0.7071067811865476
INV_ROOT = 0.3989422804014327
LANES = 128
LOGICAL = pl.DeviceIdType.LOGICAL
GROUP = 8
NN = (((1,), (0,)), ((), ()))
NT = (((1,), (1,)), ((), ()))
TN = (((0,), (0,)), ((), ()))
ROUTER, ROWS, GRADS, OUTS, DXS, HAT, MOMENT = range(7)


def mm(left_side, right_side, dims=NN):
    return lax.dot_general(left_side, right_side, dims, preferred_element_type=jnp.float32)


def gelu_parts(pre_value):
    cumulative = 0.5 * (1.0 + lax.erf(pre_value * SQRT_HALF))
    gelu_slope = cumulative + pre_value * jnp.exp(-0.5 * pre_value * pre_value) * INV_ROOT
    return (pre_value * cumulative, gelu_slope)


def layer_kernel(
    n, tile,
    images_hbm, grad_hbm, w_in_hbm, w_out_hbm, router_hbm,
    images_grad_ref, grad_in_ref, grad_out_ref, router_grad_ref,
    rows_ref, grads_ref, hidden_ref, pre_grad_ref, left_ref, right_ref,
    router_ref, images, out_grad, w_in, w_out,
    router_all, unpacked, low_packed,
    dispatch, combine, slope, stage,
    sent_a, sent_b, sent_c, sent_d, got_a, got_b, got_c, got_d,
    hat_sent, hat_got, moment_sent, moment_got,
    load_sems, send_sems, recv_sems,
):
    local, tokens, width = images.shape
    slots = n
    chunks = width // LANES
    block = local * chunks
    pack = LANES // slots
    part = router_ref.shape[0] // pack
    hidden_width = w_in.shape[1]
    me = lax.axis_index("exp") * lax.axis_size("rep") + lax.axis_index("rep")

    def load(i, source, target, pieces):
        rows = target.shape[0] // pieces
        for k in range(pieces):
            span = pl.ds(k * rows, rows)
            pltpu.make_async_copy(source.at[span], target.at[span], load_sems.at[i, k]).start()

    def loaded(i, source, target, pieces):
        rows = target.shape[0] // pieces
        for k in range(pieces):
            span = pl.ds(k * rows, rows)
            pltpu.make_async_copy(source.at[span], target.at[span], load_sems.at[i, k]).wait()

    loads = (
        (4, router_hbm, router_ref, 1),
        (0, images_hbm, images, local),
        (1, grad_hbm, out_grad, local),
        (2, w_in_hbm.at[0], w_in, 4),
        (3, w_out_hbm.at[0], w_out, 4),
    )
    load(*loads[0])

    def each_other(act):
        def one(base, step):
            half = (step + 1) // 2
            k = n // 2 + (base + half if step % 2 == 0 else -(base + half))
            other = me + k
            act(jnp.where(other >= n, other - n, other))

        def group(g, carry):
            for step in range(GROUP):
                one(g * (GROUP // 2), step)
            return carry

        groups = (n - 1) // GROUP
        lax.fori_loop(0, groups, group, 0)
        for step in range(n - 1 - groups * GROUP):
            one(groups * (GROUP // 2), step)

    barrier = pltpu.get_barrier_semaphore()

    def greet(other):
        pl.semaphore_signal(barrier, inc=1, device_id=other, device_id_type=LOGICAL)

    each_other(greet)
    for one_load in loads[1:]:
        load(*one_load)

    def exchange(phase, size, source, target, whole_source=False):
        def send(other):
            if whole_source:
                taken = source
            else:
                taken = source.at[pl.ds(pl.multiple_of(other * size, size), size)]
            pltpu.make_async_remote_copy(
                src_ref=taken,
                dst_ref=target.at[pl.ds(pl.multiple_of(me * size, size), size)],
                send_sem=send_sems.at[phase],
                recv_sem=recv_sems.at[phase],
                device_id=other,
                device_id_type=LOGICAL,
            ).start()

        each_other(send)

    def settle(sems, phase, size, target):
        span = target.at[pl.ds(0, (n - 1) * size)]
        pltpu.make_async_copy(span, span, sems.at[phase]).wait()

    loaded(*loads[0])
    own_parts = [router_ref[j * part : (j + 1) * part, :] for j in range(pack)]
    own_packed = own_parts[0] if pack == 1 else jnp.concatenate(own_parts, axis=1)
    own_router = pl.ds(pl.multiple_of(me * part, part), part)
    own_block = pl.ds(pl.multiple_of(me * block, block), block)
    router_all[own_router, :] = own_packed
    pl.semaphore_wait(barrier, n - 1)

    def send_router(other):
        pltpu.make_async_remote_copy(
            src_ref=router_all.at[own_router],
            dst_ref=router_all.at[own_router],
            send_sem=send_sems.at[ROUTER],
            recv_sem=recv_sems.at[ROUTER],
            device_id=other,
            device_id_type=LOGICAL,
        ).start()

    each_other(send_router)

    def group_sum(line):
        total = line
        for j in range(1, pack):
            total = total + pltpu.roll(line, j * slots, 1)
        return total

    settle(recv_sems, ROUTER, part, router_all)
    router_values = router_all[...]
    norm = group_sum(jnp.broadcast_to(jnp.sum(router_values * router_values, axis=0, keepdims=True), (8, LANES)))
    inv_norm = lax.rsqrt(norm + EPS)[0:1, :]
    low = (router_values * inv_norm).astype(jnp.bfloat16).astype(jnp.float32)
    low_packed[...] = low
    for j in range(pack):
        turned = low if j == 0 else pltpu.roll(low, LANES - j * slots, 1)
        unpacked[:, j * part : (j + 1) * part, :] = turned.reshape(n, part, LANES)
    router_low = jnp.transpose(unpacked[...].reshape(width, LANES))[:slots].astype(jnp.bfloat16)
    for b in range(local):
        right_ref[b, slots:, :] = router_low

    loaded(*loads[1])
    for b in range(local):
        logits = LOGIT_SCALE * mm(router_low, images[b], NT)
        powers = jnp.exp(logits - jnp.max(logits, axis=1, keepdims=True))
        soft = powers / jnp.sum(powers, axis=1, keepdims=True)
        dispatch[b] = soft
        soft_low = soft.astype(jnp.bfloat16)
        left_ref[b, :slots, :] = soft_low
        combine[b] = logits
        slot_in = mm(soft_low, images[b])
        for c in range(chunks):
            stage[pl.ds(b * chunks + c, n, stride=block), :] = slot_in[:, c * LANES : (c + 1) * LANES]
    sent_a[...] = stage[...].astype(jnp.bfloat16)
    got_a[own_block, :] = sent_a[own_block, :]
    exchange(ROWS, block, sent_a, got_a)

    loaded(*loads[2])
    for b in range(local):
        logits = combine[b]
        powers = jnp.exp(logits - jnp.max(logits, axis=0, keepdims=True))
        soft = powers / jnp.sum(powers, axis=0, keepdims=True)
        combine[b] = soft
        slot_grad = mm(soft.astype(jnp.bfloat16), out_grad[b])
        for c in range(chunks):
            stage[pl.ds(b * chunks + c, n, stride=block), :] = slot_grad[:, c * LANES : (c + 1) * LANES]
    sent_b[...] = stage[...].astype(jnp.bfloat16)
    got_b[own_block, :] = sent_b[own_block, :]
    exchange(GRADS, block, sent_b, got_b)

    def gather_rows(source, target):
        stage[...] = source[...].astype(jnp.float32)
        for c in range(chunks):
            target[:, c * LANES : (c + 1) * LANES] = stage[pl.ds(c, n * local, stride=chunks), :].astype(jnp.bfloat16)

    def spread_rows(values, target, own):
        for c in range(chunks):
            stage[pl.ds(c, n * local, stride=chunks), :] = values[:, c * LANES : (c + 1) * LANES]
        target[...] = stage[...].astype(jnp.bfloat16)
        own[own_block, :] = target[own_block, :]

    loaded(*loads[3])
    loaded(*loads[4])
    settle(recv_sems, ROWS, block, got_a)
    gather_rows(got_a, rows_ref)
    slot_rows = rows_ref[...]
    total = None
    for start in range(0, hidden_width, tile):
        span = slice(start, start + tile)
        activated, gelu_slope = gelu_parts(mm(slot_rows, w_in[:, span]))
        hidden = activated.astype(jnp.bfloat16)
        hidden_ref[:, span] = hidden
        slope[:, span] = gelu_slope
        term = mm(hidden, w_out[span, :])
        total = term if total is None else total + term
    spread_rows(total, sent_c, got_c)
    exchange(OUTS, block, sent_c, got_c)

    settle(recv_sems, GRADS, block, got_b)
    gather_rows(got_b, grads_ref)
    slot_grads = grads_ref[...]
    total = None
    for start in range(0, hidden_width, tile):
        span = slice(start, start + tile)
        pre_grad = (mm(slot_grads, w_out[span, :], NT) * slope[:, span]).astype(jnp.bfloat16)
        pre_grad_ref[:, span] = pre_grad
        term = mm(pre_grad, w_in[:, span], NT)
        total = term if total is None else total + term
    spread_rows(total, sent_d, got_d)
    exchange(DXS, block, sent_d, got_d)

    for start in range(0, hidden_width, tile):
        span = slice(start, start + tile)
        grad_out_ref[span, :] = mm(hidden_ref[:, span], slot_grads, TN).astype(jnp.bfloat16)

    def slot_values(b):
        pieces = [stage[pl.ds(b * chunks + c, n, stride=block), :] for c in range(chunks)]
        return jnp.concatenate(pieces, axis=1).astype(jnp.bfloat16)

    settle(recv_sems, OUTS, block, got_c)
    stage[...] = got_c[...].astype(jnp.float32)
    for b in range(local):
        combine_grad = mm(slot_values(b), out_grad[b], NT)
        soft = combine[b]
        combine[b] = soft * (combine_grad - jnp.sum(soft * combine_grad, axis=0, keepdims=True))

    settle(recv_sems, DXS, block, got_d)
    stage[...] = got_d[...].astype(jnp.float32)
    hat = None
    for b in range(local):
        slot_dx = slot_values(b)
        right_ref[b, :slots, :] = slot_dx
        dispatch_grad = mm(slot_dx, images[b], NT)
        soft = dispatch[b]
        grad_dispatch = soft * (dispatch_grad - jnp.sum(soft * dispatch_grad, axis=1, keepdims=True))
        logit_grad = (LOGIT_SCALE * (combine[b] + grad_dispatch)).astype(jnp.bfloat16)
        left_ref[b, slots:, :] = logit_grad
        term = mm(logit_grad, images[b])
        hat = term if hat is None else hat + term
    if slots < LANES:
        hat = jnp.concatenate((hat, jnp.zeros((LANES - slots, width), jnp.float32)), axis=0)
    unpacked[...] = jnp.transpose(hat).reshape(n, pack * part, LANES)
    packed = unpacked[:, 0:part, :].reshape(n * part, LANES)
    for j in range(1, pack):
        packed = packed + pltpu.roll(
            unpacked[:, j * part : (j + 1) * part, :].reshape(n * part, LANES), j * slots, 1
        )
    hat_sent[...] = packed
    hat_got[own_router, :] = hat_sent[own_router, :]
    exchange(HAT, part, hat_sent, hat_got)
    moment = group_sum(jnp.broadcast_to(jnp.sum(packed * low_packed[...], axis=0, keepdims=True), (8, LANES)))
    moment_sent[...] = moment[0:1, :].reshape(1, 1, LANES)
    moment_got[pl.ds(me, 1)] = moment_sent[...]
    exchange(MOMENT, 1, moment_sent, moment_got, whole_source=True)

    for b in range(local):
        images_grad_ref[b] = mm(left_ref[b], right_ref[b], TN).astype(jnp.bfloat16)
    rows_turned = jnp.transpose(rows_ref[...].astype(jnp.float32)).astype(jnp.bfloat16)
    for start in range(0, hidden_width, tile):
        span = slice(start, start + tile)
        grad_in_ref[:, span] = mm(rows_turned, pre_grad_ref[:, span]).astype(jnp.bfloat16)

    settle(recv_sems, HAT, part, hat_got)
    settle(recv_sems, MOMENT, 1, moment_got)
    hat_rows = jnp.sum(hat_got[...].reshape(n, part, LANES), axis=0)
    moment_whole = jnp.sum(moment_got[...], axis=0)
    own_hat = router_all[own_router, :] * inv_norm
    result = (hat_rows - own_hat * moment_whole) * inv_norm
    for j in range(pack):
        turned = result if j == 0 else pltpu.roll(result, LANES - j * slots, 1)
        router_grad_ref[j * part : (j + 1) * part, :] = turned[:, :slots]

    settle(send_sems, ROUTER, part, router_all)
    settle(send_sems, ROWS, block, sent_a)
    settle(send_sems, GRADS, block, sent_b)
    settle(send_sems, OUTS, block, sent_c)
    settle(send_sems, DXS, block, sent_d)
    settle(send_sems, HAT, part, hat_sent)
    settle(send_sems, MOMENT, 1, moment_got)


def drain_kernel(pieces, *refs):
    count = len(pieces)
    sources, targets, sems = refs[:count], refs[count : 2 * count], refs[-1]
    copies = []
    for source, target, cuts in zip(sources, targets, pieces):
        rows = source.shape[0] // cuts
        for k in range(cuts):
            span = pl.ds(k * rows, rows)
            copies.append(pltpu.make_async_copy(source.at[span], target.at[span], sems.at[len(copies)]))
            copies[-1].start()
    for copy in copies:
        copy.wait()


def per_device(n, rep, images, router, w_in, w_out, out_grad):
    local, tokens, width = images.shape
    hidden_width = w_in.shape[2]
    slots = router.shape[1]
    images_all = local * n
    chunks = width // LANES
    block = local * chunks
    part = router.shape[0] * slots // LANES
    low, full = jnp.bfloat16, jnp.float32
    vmem = pl.BlockSpec(memory_space=pltpu.VMEM)
    anywhere = pl.BlockSpec(memory_space=pl.ANY)
    in_hbm = pl.BlockSpec(memory_space=pltpu.HBM)
    results = (
        jax.ShapeDtypeStruct(images.shape, low),
        jax.ShapeDtypeStruct(w_in.shape[1:], low),
        jax.ShapeDtypeStruct(w_out.shape[1:], low),
        jax.ShapeDtypeStruct(router.shape, full),
    )
    made = pl.pallas_call(
        functools.partial(layer_kernel, n, 512),
        out_shape=results,
        in_specs=[in_hbm] * 5,
        out_specs=(vmem,) * 4,
        scratch_shapes=[
            pltpu.VMEM((images_all, width), low),
            pltpu.VMEM((images_all, width), low),
            pltpu.VMEM((images_all, hidden_width), low),
            pltpu.VMEM((images_all, hidden_width), low),
            pltpu.VMEM((local, 2 * slots, tokens), low),
            pltpu.VMEM((local, 2 * slots, width), low),
            pltpu.VMEM(router.shape, full),
            pltpu.VMEM((local, tokens, width), low),
            pltpu.VMEM((local, tokens, width), low),
            pltpu.VMEM((width, hidden_width), low),
            pltpu.VMEM((hidden_width, width), low),
            pltpu.VMEM((n * part, LANES), full),
            pltpu.VMEM((n, router.shape[0], LANES), full),
            pltpu.VMEM((n * part, LANES), full),
            pltpu.VMEM((local, slots, tokens), full),
            pltpu.VMEM((local, slots, tokens), full),
            pltpu.VMEM((images_all, hidden_width), full),
            pltpu.VMEM((n * block, LANES), full),
        ]
        + [pltpu.VMEM((n * block, LANES), low)] * 8
        + [
            pltpu.VMEM((n * part, LANES), full),
            pltpu.VMEM((n * part, LANES), full),
            pltpu.VMEM((1, 1, LANES), full),
            pltpu.VMEM((n, 1, LANES), full),
            pltpu.SemaphoreType.DMA((5, 4)),
            pltpu.SemaphoreType.DMA((7,)),
            pltpu.SemaphoreType.DMA((7,)),
        ],
        compiler_params=pltpu.CompilerParams(
            collective_id=0, has_side_effects=True, vmem_limit_bytes=40 * 1024 * 1024
        ),
        name="layer",
    )(*(pltpu.with_memory_space_constraint(x, pltpu.HBM) for x in (images, out_grad, w_in, w_out, router)))

    pieces = (local, 8, 8, 1)
    images_grad, grad_in, grad_out, router_grad = pl.pallas_call(
        functools.partial(drain_kernel, pieces),
        out_shape=results,
        in_specs=[anywhere] * 4,
        out_specs=(in_hbm,) * 4,
        scratch_shapes=[pltpu.SemaphoreType.DMA((sum(pieces),))],
        compiler_params=pltpu.CompilerParams(vmem_limit_bytes=2 * 1024 * 1024),
        name="drain",
    )(*made)
    return (images_grad, grad_in[None], grad_out[None], router_grad)


def solution(mesh):
    in_specs = (
        P(("exp", "rep"), None, None),
        P(("exp", "rep"), None),
        P(("exp", "rep"), None, None),
        P(("exp", "rep"), None, None),
        P(("exp", "rep"), None, None),
    )
    out_specs = (
        P(("exp", "rep"), None, None),
        P(("exp", "rep"), None, None),
        P(("exp", "rep"), None, None),
        P(("exp", "rep"), None),
    )
    rep = mesh.shape["rep"]
    n = mesh.shape["exp"] * rep
    return jax.shard_map(
        functools.partial(per_device, n, rep),
        mesh=mesh, in_specs=in_specs, out_specs=out_specs, check_vma=False,
    )
```

```python
import functools

import jax
import jax.numpy as jnp
from jax import lax
from jax.experimental import pallas as pl
from jax.experimental.pallas import tpu as pltpu
from jax.sharding import PartitionSpec as P

LOGIT_SCALE = 2.0
EPS = 1e-06
SQRT_HALF = 0.7071067811865476
INV_ROOT = 0.3989422804014327
LANES = 128
LOGICAL = pl.DeviceIdType.LOGICAL
GROUP = 8
NN = (((1,), (0,)), ((), ()))
NT = (((1,), (1,)), ((), ()))
TN = (((0,), (0,)), ((), ()))
ROUTER, ROWS, GRADS, OUTS, DXS, HAT, MOMENT, COLUMN = range(8)


def mm(left_side, right_side, dims=NN):
    return lax.dot_general(left_side, right_side, dims, preferred_element_type=jnp.float32)


def gelu_parts(pre_value):
    cumulative = 0.5 * (1.0 + lax.erf(pre_value * SQRT_HALF))
    gelu_slope = cumulative + pre_value * jnp.exp(-0.5 * pre_value * pre_value) * INV_ROOT
    return (pre_value * cumulative, gelu_slope)


def layer_kernel(
    n, tile,
    images_hbm, grad_hbm, w_in_hbm, w_out_hbm, router_hbm,
    images_grad_ref, grad_in_ref, grad_out_ref, router_grad_ref,
    rows_ref, grads_ref, hidden_ref, pre_grad_ref, left_ref, right_ref,
    router_ref, images, out_grad, w_in, w_out,
    router_all, unpacked, low_packed,
    dispatch, combine, slope, stage,
    sent_a, sent_b, sent_c, sent_d, got_a, got_b, got_c, got_d,
    hat_sent, hat_got, moment_sent, moment_got,
    load_sems, send_sems, recv_sems,
):
    local, tokens, width = images.shape
    slots = n
    chunks = width // LANES
    block = local * chunks
    pack = LANES // slots
    part = router_ref.shape[0] // pack
    hidden_width = w_in.shape[1]
    exps, reps = unpacked.shape[0], unpacked.shape[1]
    my_exp, my_rep = lax.axis_index("exp"), lax.axis_index("rep")
    me = my_exp * reps + my_rep

    def load(i, source, target, pieces):
        rows = target.shape[0] // pieces
        for k in range(pieces):
            span = pl.ds(k * rows, rows)
            pltpu.make_async_copy(source.at[span], target.at[span], load_sems.at[i, k]).start()

    def loaded(i, source, target, pieces):
        rows = target.shape[0] // pieces
        for k in range(pieces):
            span = pl.ds(k * rows, rows)
            pltpu.make_async_copy(source.at[span], target.at[span], load_sems.at[i, k]).wait()

    loads = (
        (4, router_hbm, router_ref, 1),
        (0, images_hbm, images, local),
        (1, grad_hbm, out_grad, local),
        (2, w_in_hbm.at[0], w_in, 4),
        (3, w_out_hbm.at[0], w_out, 4),
    )
    load(*loads[0])

    def each_other(act):
        def one(base, step):
            half = (step + 1) // 2
            k = n // 2 + (base + half if step % 2 == 0 else -(base + half))
            other = me + k
            act(jnp.where(other >= n, other - n, other))

        def group(g, carry):
            for step in range(GROUP):
                one(g * (GROUP // 2), step)
            return carry

        groups = (n - 1) // GROUP
        lax.fori_loop(0, groups, group, 0)
        for step in range(n - 1 - groups * GROUP):
            one(groups * (GROUP // 2), step)

    barrier = pltpu.get_barrier_semaphore()

    def greet(other):
        pl.semaphore_signal(barrier, inc=1, device_id=other, device_id_type=LOGICAL)

    each_other(greet)
    for one_load in loads[1:]:
        load(*one_load)

    def exchange(phase, size, source, target, whole_source=False):
        def send(other):
            if whole_source:
                taken = source
            else:
                taken = source.at[pl.ds(pl.multiple_of(other * size, size), size)]
            pltpu.make_async_remote_copy(
                src_ref=taken,
                dst_ref=target.at[pl.ds(pl.multiple_of(me * size, size), size)],
                send_sem=send_sems.at[phase],
                recv_sem=recv_sems.at[phase],
                device_id=other,
                device_id_type=LOGICAL,
            ).start()

        each_other(send)

    def settle(sems, phase, size, target):
        span = target.at[pl.ds(0, (n - 1) * size)]
        pltpu.make_async_copy(span, span, sems.at[phase]).wait()

    loaded(*loads[0])
    own_parts = [router_ref[j * part : (j + 1) * part, :] for j in range(pack)]
    own_packed = own_parts[0] if pack == 1 else jnp.concatenate(own_parts, axis=1)
    own_router = pl.ds(pl.multiple_of(me * part, part), part)
    own_block = pl.ds(pl.multiple_of(me * block, block), block)
    own_tile = pl.ds(pl.multiple_of((my_rep * exps + my_exp) * part, part), part)
    own_column = pl.ds(pl.multiple_of(my_rep * exps * part, exps * part), exps * part)
    router_all[own_tile, :] = own_packed
    pl.semaphore_wait(barrier, n - 1)

    def send_router(span, phase, other):
        pltpu.make_async_remote_copy(
            src_ref=router_all.at[span],
            dst_ref=router_all.at[span],
            send_sem=send_sems.at[phase],
            recv_sem=recv_sems.at[phase],
            device_id=other,
            device_id_type=LOGICAL,
        ).start()

    def router_done(sems, phase, rows):
        span = router_all.at[pl.ds(0, rows)]
        pltpu.make_async_copy(span, span, sems.at[phase]).wait()

    tile_rows, column_rows = (exps - 1) * part, (reps - 1) * exps * part
    for k in range(1, exps):
        send_router(own_tile, ROUTER, lax.rem(my_exp + k, exps) * reps + my_rep)
    router_done(recv_sems, ROUTER, tile_rows)
    for k in range(1, reps):
        send_router(own_column, COLUMN, my_exp * reps + lax.rem(my_rep + k, reps))
    router_done(recv_sems, COLUMN, column_rows)

    def group_sum(line):
        total = line
        for j in range(1, pack):
            total = total + pltpu.roll(line, j * slots, 1)
        return total

    router_values = router_all[...]
    norm = group_sum(jnp.broadcast_to(jnp.sum(router_values * router_values, axis=0, keepdims=True), (8, LANES)))
    inv_norm = lax.rsqrt(norm + EPS)[0:1, :]
    low = (router_values * inv_norm).astype(jnp.bfloat16).astype(jnp.float32)
    for q in range(reps):
        low_packed[:, q] = low.reshape(reps, exps, part, LANES)[q]
    for j in range(pack):
        turned = low if j == 0 else pltpu.roll(low, LANES - j * slots, 1)
        turned = turned.reshape(reps, exps, part, LANES)
        for q in range(reps):
            unpacked[:, q, j * part : (j + 1) * part, :] = turned[q]
    router_low = jnp.transpose(unpacked[...].reshape(width, LANES))[:slots].astype(jnp.bfloat16)
    for b in range(local):
        right_ref[b, slots:, :] = router_low

    loaded(*loads[1])
    for b in range(local):
        logits = LOGIT_SCALE * mm(router_low, images[b], NT)
        powers = jnp.exp(logits - jnp.max(logits, axis=1, keepdims=True))
        soft = powers / jnp.sum(powers, axis=1, keepdims=True)
        dispatch[b] = soft
        soft_low = soft.astype(jnp.bfloat16)
        left_ref[b, :slots, :] = soft_low
        combine[b] = logits
        slot_in = mm(soft_low, images[b])
        for c in range(chunks):
            stage[pl.ds(b * chunks + c, n, stride=block), :] = slot_in[:, c * LANES : (c + 1) * LANES]
    sent_a[...] = stage[...].astype(jnp.bfloat16)
    got_a[own_block, :] = sent_a[own_block, :]
    exchange(ROWS, block, sent_a, got_a)

    loaded(*loads[2])
    for b in range(local):
        logits = combine[b]
        powers = jnp.exp(logits - jnp.max(logits, axis=0, keepdims=True))
        soft = powers / jnp.sum(powers, axis=0, keepdims=True)
        combine[b] = soft
        slot_grad = mm(soft.astype(jnp.bfloat16), out_grad[b])
        for c in range(chunks):
            stage[pl.ds(b * chunks + c, n, stride=block), :] = slot_grad[:, c * LANES : (c + 1) * LANES]
    sent_b[...] = stage[...].astype(jnp.bfloat16)
    got_b[own_block, :] = sent_b[own_block, :]
    exchange(GRADS, block, sent_b, got_b)

    def gather_rows(source, target):
        stage[...] = source[...].astype(jnp.float32)
        for c in range(chunks):
            target[:, c * LANES : (c + 1) * LANES] = stage[pl.ds(c, n * local, stride=chunks), :].astype(jnp.bfloat16)

    def spread_rows(values, target, own):
        for c in range(chunks):
            stage[pl.ds(c, n * local, stride=chunks), :] = values[:, c * LANES : (c + 1) * LANES]
        target[...] = stage[...].astype(jnp.bfloat16)
        own[own_block, :] = target[own_block, :]

    loaded(*loads[3])
    loaded(*loads[4])
    settle(recv_sems, ROWS, block, got_a)
    gather_rows(got_a, rows_ref)
    slot_rows = rows_ref[...]
    total = None
    for start in range(0, hidden_width, tile):
        span = slice(start, start + tile)
        activated, gelu_slope = gelu_parts(mm(slot_rows, w_in[:, span]))
        hidden = activated.astype(jnp.bfloat16)
        hidden_ref[:, span] = hidden
        slope[:, span] = gelu_slope
        term = mm(hidden, w_out[span, :])
        total = term if total is None else total + term
    spread_rows(total, sent_c, got_c)
    exchange(OUTS, block, sent_c, got_c)

    settle(recv_sems, GRADS, block, got_b)
    gather_rows(got_b, grads_ref)
    slot_grads = grads_ref[...]
    total = None
    for start in range(0, hidden_width, tile):
        span = slice(start, start + tile)
        pre_grad = (mm(slot_grads, w_out[span, :], NT) * slope[:, span]).astype(jnp.bfloat16)
        pre_grad_ref[:, span] = pre_grad
        term = mm(pre_grad, w_in[:, span], NT)
        total = term if total is None else total + term
    spread_rows(total, sent_d, got_d)
    exchange(DXS, block, sent_d, got_d)

    for start in range(0, hidden_width, tile):
        span = slice(start, start + tile)
        grad_out_ref[span, :] = mm(hidden_ref[:, span], slot_grads, TN).astype(jnp.bfloat16)

    def slot_values(b):
        pieces = [stage[pl.ds(b * chunks + c, n, stride=block), :] for c in range(chunks)]
        return jnp.concatenate(pieces, axis=1).astype(jnp.bfloat16)

    settle(recv_sems, OUTS, block, got_c)
    stage[...] = got_c[...].astype(jnp.float32)
    for b in range(local):
        combine_grad = mm(slot_values(b), out_grad[b], NT)
        soft = combine[b]
        combine[b] = soft * (combine_grad - jnp.sum(soft * combine_grad, axis=0, keepdims=True))

    settle(recv_sems, DXS, block, got_d)
    stage[...] = got_d[...].astype(jnp.float32)
    hat = None
    for b in range(local):
        slot_dx = slot_values(b)
        right_ref[b, :slots, :] = slot_dx
        dispatch_grad = mm(slot_dx, images[b], NT)
        soft = dispatch[b]
        grad_dispatch = soft * (dispatch_grad - jnp.sum(soft * dispatch_grad, axis=1, keepdims=True))
        logit_grad = (LOGIT_SCALE * (combine[b] + grad_dispatch)).astype(jnp.bfloat16)
        left_ref[b, slots:, :] = logit_grad
        term = mm(logit_grad, images[b])
        hat = term if hat is None else hat + term
    if slots < LANES:
        hat = jnp.concatenate((hat, jnp.zeros((LANES - slots, width), jnp.float32)), axis=0)
    unpacked[...] = jnp.transpose(hat).reshape(exps, reps, pack * part, LANES)
    packed = unpacked[:, :, 0:part, :].reshape(n * part, LANES)
    for j in range(1, pack):
        packed = packed + pltpu.roll(
            unpacked[:, :, j * part : (j + 1) * part, :].reshape(n * part, LANES), j * slots, 1
        )
    hat_sent[...] = packed
    hat_got[own_router, :] = hat_sent[own_router, :]
    exchange(HAT, part, hat_sent, hat_got)
    moment = group_sum(jnp.broadcast_to(jnp.sum(packed * low_packed[...].reshape(n * part, LANES), axis=0, keepdims=True), (8, LANES)))
    moment_sent[...] = moment[0:1, :].reshape(1, 1, LANES)
    moment_got[pl.ds(me, 1)] = moment_sent[...]
    exchange(MOMENT, 1, moment_sent, moment_got, whole_source=True)

    for b in range(local):
        images_grad_ref[b] = mm(left_ref[b], right_ref[b], TN).astype(jnp.bfloat16)
    rows_turned = jnp.transpose(rows_ref[...].astype(jnp.float32)).astype(jnp.bfloat16)
    for start in range(0, hidden_width, tile):
        span = slice(start, start + tile)
        grad_in_ref[:, span] = mm(rows_turned, pre_grad_ref[:, span]).astype(jnp.bfloat16)

    settle(recv_sems, HAT, part, hat_got)
    settle(recv_sems, MOMENT, 1, moment_got)
    hat_rows = jnp.sum(hat_got[...].reshape(n, part, LANES), axis=0)
    moment_whole = jnp.sum(moment_got[...], axis=0)
    own_hat = router_all[own_tile, :] * inv_norm
    result = (hat_rows - own_hat * moment_whole) * inv_norm
    for j in range(pack):
        turned = result if j == 0 else pltpu.roll(result, LANES - j * slots, 1)
        router_grad_ref[j * part : (j + 1) * part, :] = turned[:, :slots]

    router_done(send_sems, ROUTER, tile_rows)
    router_done(send_sems, COLUMN, column_rows)
    settle(send_sems, ROWS, block, sent_a)
    settle(send_sems, GRADS, block, sent_b)
    settle(send_sems, OUTS, block, sent_c)
    settle(send_sems, DXS, block, sent_d)
    settle(send_sems, HAT, part, hat_sent)
    settle(send_sems, MOMENT, 1, moment_got)


def drain_kernel(pieces, *refs):
    count = len(pieces)
    sources, targets, sems = refs[:count], refs[count : 2 * count], refs[-1]
    copies = []
    for source, target, cuts in zip(sources, targets, pieces):
        rows = source.shape[0] // cuts
        for k in range(cuts):
            span = pl.ds(k * rows, rows)
            copies.append(pltpu.make_async_copy(source.at[span], target.at[span], sems.at[len(copies)]))
            copies[-1].start()
    for copy in copies:
        copy.wait()


def per_device(n, rep, images, router, w_in, w_out, out_grad):
    local, tokens, width = images.shape
    hidden_width = w_in.shape[2]
    slots = router.shape[1]
    images_all = local * n
    chunks = width // LANES
    block = local * chunks
    part = router.shape[0] * slots // LANES
    low, full = jnp.bfloat16, jnp.float32
    vmem = pl.BlockSpec(memory_space=pltpu.VMEM)
    anywhere = pl.BlockSpec(memory_space=pl.ANY)
    in_hbm = pl.BlockSpec(memory_space=pltpu.HBM)
    results = (
        jax.ShapeDtypeStruct(images.shape, low),
        jax.ShapeDtypeStruct(w_in.shape[1:], low),
        jax.ShapeDtypeStruct(w_out.shape[1:], low),
        jax.ShapeDtypeStruct(router.shape, full),
    )
    made = pl.pallas_call(
        functools.partial(layer_kernel, n, 512),
        out_shape=results,
        in_specs=[in_hbm] * 5,
        out_specs=(vmem,) * 4,
        scratch_shapes=[
            pltpu.VMEM((images_all, width), low),
            pltpu.VMEM((images_all, width), low),
            pltpu.VMEM((images_all, hidden_width), low),
            pltpu.VMEM((images_all, hidden_width), low),
            pltpu.VMEM((local, 2 * slots, tokens), low),
            pltpu.VMEM((local, 2 * slots, width), low),
            pltpu.VMEM(router.shape, full),
            pltpu.VMEM((local, tokens, width), low),
            pltpu.VMEM((local, tokens, width), low),
            pltpu.VMEM((width, hidden_width), low),
            pltpu.VMEM((hidden_width, width), low),
            pltpu.VMEM((n * part, LANES), full),
            pltpu.VMEM((n // rep, rep, router.shape[0], LANES), full),
            pltpu.VMEM((n // rep, rep, part, LANES), full),
            pltpu.VMEM((local, slots, tokens), full),
            pltpu.VMEM((local, slots, tokens), full),
            pltpu.VMEM((images_all, hidden_width), full),
            pltpu.VMEM((n * block, LANES), full),
        ]
        + [pltpu.VMEM((n * block, LANES), low)] * 8
        + [
            pltpu.VMEM((n * part, LANES), full),
            pltpu.VMEM((n * part, LANES), full),
            pltpu.VMEM((1, 1, LANES), full),
            pltpu.VMEM((n, 1, LANES), full),
            pltpu.SemaphoreType.DMA((5, 4)),
            pltpu.SemaphoreType.DMA((8,)),
            pltpu.SemaphoreType.DMA((8,)),
        ],
        compiler_params=pltpu.CompilerParams(
            collective_id=0, has_side_effects=True, vmem_limit_bytes=40 * 1024 * 1024
        ),
        name="layer",
    )(*(pltpu.with_memory_space_constraint(x, pltpu.HBM) for x in (images, out_grad, w_in, w_out, router)))

    pieces = (local, 8, 8, 1)
    images_grad, grad_in, grad_out, router_grad = pl.pallas_call(
        functools.partial(drain_kernel, pieces),
        out_shape=results,
        in_specs=[anywhere] * 4,
        out_specs=(in_hbm,) * 4,
        scratch_shapes=[pltpu.SemaphoreType.DMA((sum(pieces),))],
        compiler_params=pltpu.CompilerParams(vmem_limit_bytes=2 * 1024 * 1024),
        name="drain",
    )(*made)
    return (images_grad, grad_in[None], grad_out[None], router_grad)


def solution(mesh):
    in_specs = (
        P(("exp", "rep"), None, None),
        P(("exp", "rep"), None),
        P(("exp", "rep"), None, None),
        P(("exp", "rep"), None, None),
        P(("exp", "rep"), None, None),
    )
    out_specs = (
        P(("exp", "rep"), None, None),
        P(("exp", "rep"), None, None),
        P(("exp", "rep"), None, None),
        P(("exp", "rep"), None),
    )
    rep = mesh.shape["rep"]
    n = mesh.shape["exp"] * rep
    return jax.shard_map(
        functools.partial(per_device, n, rep),
        mesh=mesh, in_specs=in_specs, out_specs=out_specs, check_vma=False,
    )
```
